256 devices in a mesh: cls: 4 (over x_hi, core), ptl: 64 (over x_lo, y, z).
Axes of the slice: x: 4 (x_hi: 2, x_lo: 2; x = x_hi * 2 + x_lo), y: 4, z: 8, core: 2. Of those that a mesh axis runs over, the one named last changes fastest.
Arguments:
- particles: bfloat16 [512, 12288], P(('cls', 'ptl')), may hold values from -8 to 8
- references: bfloat16 [100, 12288], P('cls'), may hold values from -1 to 1
- centers: int32 [512, 2], P(('cls', 'ptl')), may hold values from -3 to 3
- rot_prior: int32 [512], P(('cls', 'ptl')), may hold values from 0 to 11
- groups: int32 [512], P(('cls', 'ptl')), may hold values from 0 to 15
- class_frac: float32 [100], replicated, may hold values from 0.002 to 0.03
- inv_noise: float32 [16, 32], replicated, may hold values from 0.5 to 2
- reg_inv: float32 [32], replicated, may hold values from 1 to 8
Outputs:
- new_refs: float32 [100, 12288], P('cls')
- new_frac: float32 [100], P('cls')
- log_evidence: float32 [512], P(('cls', 'ptl'))
The draws below stay inside these ranges and needn't reach their ends.
All inputs are finite; a program needn't handle non-finite values.
Results may differ from the reference program's by a relative error of at most 0.002.
Values may be sent and summed in bfloat16 or wider, within the bound.
A program may use at most 128 MiB of HBM per device.

```python
import math
import jax
import jax.numpy as jnp
from jax import lax

CLASSES = 100
ROTS = 12
SHIFT_SPAN = 2
CYCLES = 32
ANGLES = 192
BOX = 128
GROUPS = 16
SHIFTS = 25
FEAT = 12288
ROT_STEP = 16
NP = 512


def reference_values(key):
    values = jax.random.normal(jax.random.fold_in(key, 11), (CLASSES, FEAT), jnp.float32)
    values = jnp.clip(values, -4.0, 4.0) * (3.0 / FEAT ** 0.5)
    return jnp.clip(values, -1.0, 1.0)


def draw_references(key, part):
    return reference_values(key).astype(jnp.bfloat16)


def draw_particles(key, part):
    noise_part = jnp.clip(jax.random.normal(jax.random.fold_in(key, 13), (NP, FEAT), jnp.float32), -6.0, 6.0)
    return jnp.clip(noise_part, -8.0, 8.0).astype(jnp.bfloat16)


def plant(drawn, stream_key, least, top_value):
    index_at = [jax.random.randint(jax.random.fold_in(stream_key, axis), (), 0, length) for axis, length in enumerate(drawn.shape)]
    widest = drawn.shape.index(max(drawn.shape))
    beside = index_at[:widest] + [(index_at[widest] + 1) % drawn.shape[widest]] + index_at[widest + 1:]
    return drawn.at[tuple(index_at)].set(least).at[tuple(beside)].set(top_value)


def setup_inputs(seed: int = 0) -> dict:
    splits = jax.random.split(jax.random.key(seed), 9)
    particles = draw_particles(jax.random.fold_in(splits[8], 71), 0)
    references = draw_references(jax.random.fold_in(splits[8], 71), 0)
    centers = plant(jax.random.randint(splits[2], (NP, 2), -3, 4), jax.random.fold_in(splits[2], 1), -3, 3).astype(jnp.int32)
    rot_prior = plant(jax.random.randint(splits[3], (NP,), 0, ROTS), jax.random.fold_in(splits[3], 1), 0, ROTS - 1).astype(jnp.int32)
    groups = plant(jax.random.randint(splits[4], (NP,), 0, GROUPS), jax.random.fold_in(splits[4], 1), 0, GROUPS - 1).astype(jnp.int32)
    class_frac = jnp.clip(jnp.exp(jax.random.uniform(splits[5], (CLASSES,), jnp.float32, math.log(0.002), math.log(0.03))), 0.002, 0.03)
    inv_noise = jnp.clip(jnp.exp(jax.random.uniform(splits[6], (GROUPS, CYCLES), jnp.float32, math.log(0.5), math.log(2.0))), 0.5, 2.0)
    reg_inv = jnp.clip(jnp.exp(jax.random.uniform(splits[7], (CYCLES,), jnp.float32, math.log(1.0), math.log(8.0))), 1.0, 8.0)
    return {"particles": particles, "references": references, "centers": centers, "rot_prior": rot_prior, "groups": groups, "class_frac": class_frac, "inv_noise": inv_noise, "reg_inv": reg_inv}


KAPPA = 0.25
HIGHEST = lax.Precision.HIGHEST


def freq_tables():
    cycle_ids = jnp.arange(CYCLES, dtype=jnp.float32) + 1.0
    angle_grid = jnp.arange(ANGLES, dtype=jnp.float32) * (2.0 * math.pi / ANGLES)
    freq_x = cycle_ids[:, None] * jnp.cos(angle_grid)[None, :] / BOX
    freq_y = cycle_ids[:, None] * jnp.sin(angle_grid)[None, :] / BOX
    return freq_x, freq_y


def aligned_images(images, centers, inv_rows, shift_index, freq_x, freq_y):
    shift_side = 2 * SHIFT_SPAN + 1
    move_x = centers[:, 0] + shift_index // shift_side - SHIFT_SPAN
    move_y = centers[:, 1] + shift_index % shift_side - SHIFT_SPAN
    phase_grid = (2.0 * math.pi) * (move_x.astype(jnp.float32)[:, None, None] * freq_x + move_y.astype(jnp.float32)[:, None, None] * freq_y)
    cosine_grid = jnp.cos(phase_grid)
    sine_grid = jnp.sin(phase_grid)
    real_part = images[:, 0] * cosine_grid - images[:, 1] * sine_grid
    imag_part = images[:, 0] * sine_grid + images[:, 1] * cosine_grid
    weight = inv_rows[:, :, None]
    return jnp.stack([real_part * weight, imag_part * weight], axis=1).astype(jnp.bfloat16)


def rotated_rows(aligned, first_rot, number):
    row_count = aligned.shape[0]
    return jnp.concatenate([jnp.roll(aligned, -(first_rot + rotation) * ROT_STEP, axis=3).reshape(row_count, FEAT) for rotation in range(number)], axis=0)


def prior_term(rot_prior):
    rotation_ids = jnp.arange(ROTS, dtype=jnp.int32)
    distance = (rotation_ids[:, None] - rot_prior[None, :]) % ROTS
    distance = jnp.minimum(distance, ROTS - distance).astype(jnp.float32)
    return -KAPPA * distance * distance


def cycle_power(references):
    values = references.astype(jnp.float32).reshape(references.shape[0], 2, CYCLES, ANGLES)
    return jnp.sum(values * values, axis=(1, 3))


def reference(particles, references, centers, rot_prior, groups, class_frac, inv_noise, reg_inv):
    freq_x, freq_y = freq_tables()
    cycle_sums = cycle_power(references)
    log_frac = jnp.log(class_frac)
    block_rows = math.gcd(NP, 64)
    block_count = NP // block_rows
    shift_ids = jnp.arange(SHIFTS, dtype=jnp.int32)

    def per_block(carry_value, inputs):
        numerator, denominator, fraction = carry_value
        block_images, block_centers, block_prior, block_groups = inputs
        images = block_images.astype(jnp.float32).reshape(block_rows, 2, CYCLES, ANGLES)
        inv_rows = inv_noise[block_groups]
        penalty = jnp.dot(inv_rows, cycle_sums.T, precision=HIGHEST)
        score_bias = (-0.5 * penalty)[None] + log_frac[None, None, :] + prior_term(block_prior)[:, :, None]

        def shift_scores(unused_carry, shift_index):
            aligned = aligned_images(images, block_centers, inv_rows, shift_index, freq_x, freq_y)
            stacked = rotated_rows(aligned, 0, ROTS)
            raw_scores = jnp.dot(stacked, references.T, preferred_element_type=jnp.float32)
            return unused_carry, raw_scores.reshape(ROTS, block_rows, CLASSES) + score_bias

        _, scores = lax.scan(shift_scores, jnp.int32(0), shift_ids)
        peak = jnp.max(scores, axis=(0, 1, 3))
        exp_terms = jnp.exp(scores - peak[None, None, :, None])
        summed = jnp.sum(exp_terms, axis=(0, 1, 3))
        evidence = peak + jnp.log(summed)
        posterior = exp_terms / summed[None, None, :, None]
        rounded = posterior.astype(jnp.bfloat16)
        per_class = jnp.sum(posterior, axis=(0, 1))
        denominator = denominator + jnp.dot(per_class.T, inv_rows, precision=HIGHEST)
        fraction = fraction + jnp.sum(per_class, axis=0)

        def add_shift(running, shift_inputs):
            shift_index, shift_weights = shift_inputs
            aligned = aligned_images(images, block_centers, inv_rows, shift_index, freq_x, freq_y)
            stacked = rotated_rows(aligned, 0, ROTS)
            portion = shift_weights.reshape(ROTS * block_rows, CLASSES)
            return running + lax.dot_general(portion, stacked, (((0,), (0,)), ((), ())), preferred_element_type=jnp.float32), None

        numerator, _ = lax.scan(add_shift, numerator, (shift_ids, rounded))
        return (numerator, denominator, fraction), evidence

    initial = (jnp.zeros((CLASSES, FEAT), jnp.float32), jnp.zeros((CLASSES, CYCLES), jnp.float32), jnp.zeros((CLASSES,), jnp.float32))
    inputs = (particles.reshape(block_count, block_rows, FEAT), centers.reshape(block_count, block_rows, 2), rot_prior.reshape(block_count, block_rows), groups.reshape(block_count, block_rows))
    (numerator, denominator, fraction), evidence = lax.scan(per_block, initial, inputs)
    divisor = denominator + reg_inv[None, :]
    spread = jnp.broadcast_to(divisor[:, None, :, None], (CLASSES, 2, CYCLES, ANGLES)).reshape(CLASSES, FEAT)
    new_refs = numerator / spread
    new_frac = fraction / NP
    return new_refs, new_frac, evidence.reshape(NP)
```

```python
import math

import jax
import jax.numpy as jnp
import numpy as np
from jax import lax
from jax.experimental import pallas as pl
from jax.experimental.pallas import tpu as pltpu
from jax.sharding import PartitionSpec as P

ROTS = 12
SPAN = 2
CYCLES = 32
ANGLES = 192
BOX = 128
SHIFTS = 25
FEAT = 12288
KAPPA = 0.25
HIGHEST = lax.Precision.HIGHEST
MESH = pl.DeviceIdType.MESH
F32, BF16 = jnp.float32, jnp.bfloat16

KPAD = 32
ROWS = 304
SLOT = 48


def tables():
    cycle = np.arange(CYCLES, dtype=np.float64) + 1.0
    angle = np.arange(ANGLES, dtype=np.float64) * (2.0 * math.pi / ANGLES)
    fx = cycle[:, None] * np.cos(angle)[None] / BOX
    fy = cycle[:, None] * np.sin(angle)[None] / BOX

    def blocked(v):
        n = v.shape[0]
        v = v.reshape(n, 4, 8, 12, 16)
        return np.transpose(v, (3, 0, 1, 2, 4)).reshape(12, n, 512)

    t = np.arange(SHIFTS)
    mx, my = t // 5 - SPAN, t % 5 - SPAN
    ph = 2.0 * math.pi * (mx[:, None, None] * fx + my[:, None, None] * fy)
    shift = np.concatenate([np.cos(ph), np.zeros((7, 32, 192)), np.sin(ph), np.zeros((7, 32, 192))])
    rows = []
    for f in (fx, fy):
        for m in (1, 2, 3):
            rows += [np.cos(2.0 * math.pi * m * f), np.sin(2.0 * math.pi * m * f)]
    center = np.stack(rows + [np.zeros_like(fx)] * 4)
    return blocked(shift).astype(np.float32), blocked(center).astype(np.float32)


def shard_maps():
    spread = np.zeros((128, 1024), np.float32)
    for rho in range(8):
        for j in range(8):
            for s in range(16):
                spread[rho * 16 + s, rho * 128 + j * 16 + s] = 1
    rows = np.zeros((SLOT, 8 * SLOT), np.float32)
    for rho in range(8):
        for k in range(4):
            for b in range(12):
                rows[k * 12 + (12 * rho + b) // 8, rho * SLOT + k * 12 + b] = 1
    return spread, rows


def to_blocks(nat):
    lane = lax.broadcasted_iota(jnp.int32, nat[0].shape, 1) // 16
    out = []
    for b in range(12):
        acc = None
        for rho in range(8):
            n, j = divmod(12 * rho + b, 8)
            v = nat[n] if j == rho else pltpu.roll(nat[n], (16 * (rho - j)) % 128, 1)
            acc = v if acc is None else jnp.where(lane == rho, v, acc)
        out.append(acc)
    return out


def fold(v, op):
    v = jnp.broadcast_to(op(v[:, :128], v[:, 128:]), (8, 128))
    for step in (8, 16, 32, 64):
        v = op(v, pltpu.roll(v, step, 1))
    return v


def encode(value, to):
    top = jnp.max(jnp.abs(value), axis=0, keepdims=True)
    power = jnp.ceil(jnp.log2(jnp.maximum(top, 1e-30)) + 1e-3) - 15.0
    code = jnp.round(value * jnp.exp2(-power))
    row = lax.broadcasted_iota(jnp.int32, value.shape, 0)
    to[...] = jnp.where(row == 300, power, code).astype(jnp.int32).astype(jnp.int16)


def decode(code):
    value = code[...].astype(jnp.int32).astype(F32)
    return value * jnp.exp2(value[300:301])


def kernel(
    x_ref, cen_ref, rot_ref, group_ref, frac_in, noise_ref, reg_ref,
    refs_hbm, shift_hbm, center_hbm, spread_hbm, rows_hbm,
    out_ref, frac_ref, evid_ref,
    refs_ref, shift_ref, center_ref, spread_ref, rows_ref,
    xs, ms, xb, xg, mg, xf, yre, yim, a_ref, r2, pw, s_ref, sm_src, sm, p2, n_ref, nb, sb, rs1, acc,
    ph2, rs2, ag1, ag2s, ag2, fin, dsrc, dz, dpsrc, dp, in_s,
    x_s, x_r, m_s, m_r, sm_s, sm_r, rs1_s, rs1_r, rs2_s, rs2_r, ag1_s, ag1_r, ag2_s, ag2_r,
    dz_s, dz_r, dp_s, dp_r,
):
    c = lax.axis_index("cls")
    q = lax.axis_index("ptl")
    h, z = q // 8, q % 8

    def at_cls(d):
        return ((c + d) % 4, q)

    def at_z(d):
        return (c, h * 8 + (z + d) % 8)

    def at_plane(d):
        return (c, ((h + d) % 8) * 8 + z)

    loads = [
        pltpu.make_async_copy(src, dst, in_s.at[i])
        for i, (src, dst) in enumerate(
            (
                (refs_hbm, refs_ref), (center_hbm, center_ref), (shift_hbm, shift_ref),
                (spread_hbm, spread_ref), (rows_hbm, rows_ref),
            )
        )
    ]
    for load in loads:
        load.start()
    barrier = pltpu.get_barrier_semaphore()
    for d in range(1, 4):
        pl.semaphore_signal(barrier, inc=1, device_id=at_cls(d), device_id_type=MESH)
    for d in range(1, 8):
        pl.semaphore_signal(barrier, inc=1, device_id=at_z(d), device_id_type=MESH)
        pl.semaphore_signal(barrier, inc=1, device_id=at_plane(d), device_id_type=MESH)

    lane1 = lax.broadcasted_iota(jnp.int32, (1, 128), 1)
    ms[...] = jnp.zeros_like(ms)
    for p in range(2):
        for g in range(8):
            xs[p * 8 + g : p * 8 + g + 1, :] = x_ref[p : p + 1, g * 1536 : (g + 1) * 1536].astype(F32)
        group = lax.broadcasted_iota(jnp.int32, (16, CYCLES), 0) == group_ref[p]
        inv = jnp.sum(jnp.where(group, noise_ref[...], 0.0), axis=0, keepdims=True)
        info = jnp.concatenate([inv, jnp.ones((1, 96), F32)], axis=1)
        for at, value in ((40, cen_ref[p, 0]), (41, cen_ref[p, 1]), (42, rot_ref[p])):
            info = jnp.where(lane1 == at, value.astype(F32), info)
        ms[p * 4 : p * 4 + 1, :] = info
    xb[...] = xs[...].astype(BF16)
    pl.semaphore_wait(barrier, 17)

    def remote(src, dst, ss, rs, dev):
        return pltpu.make_async_remote_copy(
            src_ref=src, dst_ref=dst, send_sem=ss, recv_sem=rs, device_id=dev, device_id_type=MESH
        )

    x_copies = []
    for d in range(1, 4):
        x_copies.append(remote(ms, mg.at[c], m_s.at[d], m_r.at[d], at_cls(d)))
        x_copies.append(remote(xb, xg.at[c], x_s.at[d], x_r.at[d], at_cls(d)))
    for copy in x_copies:
        copy.start()
    xg[c] = xb[...]
    mg[c] = ms[...]
    loads[0].wait()

    pw[...] = jnp.zeros_like(pw)

    def one_group(g, carry):
        at = pl.multiple_of(g * 1536, 1536)
        nat = [refs_ref[:, pl.ds(at + n * 128, 128)].astype(F32) for n in range(12)]
        blocks = to_blocks(nat)
        power = blocks[0] * blocks[0]
        for b in range(1, 12):
            power = power + blocks[b] * blocks[b]
        to = pl.multiple_of(g * 128, 128)
        pw[0:25, pl.ds(pl.multiple_of((g % 4) * 128, 128), 128)] += power
        for b in range(12):
            v = blocks[b].astype(BF16)
            j = (12 - b) % 12
            r2[j * 32 : j * 32 + 25, pl.ds(to, 128)] = v
            r2[(j + 12) * 32 : (j + 12) * 32 + 25, pl.ds(to, 128)] = v
        return carry

    lax.fori_loop(0, 8, one_group, 0)
    a_ref[:, 200:256, :] = jnp.zeros((12, 56, 1024), BF16)
    s_ref[...] = jnp.zeros_like(s_ref)
    nb[...] = jnp.zeros_like(nb)
    ph2[...] = jnp.zeros_like(ph2)

    loads[1].wait()
    loads[2].wait()
    for copy in x_copies:
        copy.wait()

    for i in range(4):
        for n in range(12):
            at = n * 64 + i * 16
            xf[at : at + 16, :] = xg[i, :, n * 128 : n * 128 + 128].astype(F32)
    for i in range(4):
        fin[i * 8 : i * 8 + 8, :] = mg[i]
    info = fin[pl.ds(0, 8, stride=4), :]
    lane8 = lax.broadcasted_iota(jnp.int32, (8, 128), 1)
    cx, cy = info[:, 40:41], info[:, 41:42]
    turn = jnp.where(lane8 % 8 == lax.broadcasted_iota(jnp.int32, (8, 128), 0), info[:, 42:43], 0.0)
    turn = jnp.sum(turn, axis=0, keepdims=True)
    grow = (
        lax.broadcasted_iota(jnp.int32, (CYCLES, 512), 0)
        == lax.broadcasted_iota(jnp.int32, (CYCLES, 512), 1) // 16
    ).astype(F32)
    w512 = jnp.dot(info[:, 0:CYCLES], grow, preferred_element_type=F32, precision=HIGHEST)
    w = [w512[:, i * 128 : i * 128 + 128] for i in range(4)]

    def phase(value, row, b, gq):
        size = jnp.abs(value)
        cos, sin = jnp.ones((8, 128), F32), jnp.zeros((8, 128), F32)
        for m in (1, 2, 3):
            hit = size == float(m)
            at = row + (m - 1) * 2
            cos = jnp.where(hit, center_ref[b, at : at + 1, gq * 128 : gq * 128 + 128], cos)
            sin = jnp.where(hit, center_ref[b, at + 1 : at + 2, gq * 128 : gq * 128 + 128], sin)
        return cos, jnp.where(value < 0.0, -sin, sin)

    for gq in range(4):
        re = to_blocks([xf[pl.ds(n * 64 + gq, 8, stride=8), :] for n in range(12)])
        im = to_blocks([xf[pl.ds(n * 64 + gq + 4, 8, stride=8), :] for n in range(12)])
        for b in range(12):
            xc, xs = phase(cx, 0, b, gq)
            yc, ys = phase(cy, 6, b, gq)
            pc, ps = xc * yc - xs * ys, xc * ys + xs * yc
            u, v = re[b] * w[gq], im[b] * w[gq]
            yre[b, :, gq * 128 : gq * 128 + 128] = u * pc - v * ps
            yim[b, :, gq * 128 : gq * 128 + 128] = u * ps + v * pc

    def one_block(b, carry):
        for l in range(4):
            cols = slice(l * 128, l * 128 + 128)
            u, v = yre[b, :, cols], yim[b, :, cols]
            for t in range(0, 25, 2):
                res, ims = [], []
                for tt in range(t, min(t + 2, 25)):
                    tc = shift_ref[b, tt : tt + 1, cols]
                    ts = shift_ref[b, 32 + tt : 33 + tt, cols]
                    res.append(u * tc - v * ts)
                    ims.append(u * ts + v * tc)
                if len(res) == 1:
                    res.append(jnp.zeros((8, 128), F32))
                    ims.append(jnp.zeros((8, 128), F32))
                at = slice(t * 8, t * 8 + 16)
                a_ref[b, at, cols] = jnp.concatenate(res, axis=0).astype(BF16)
                a_ref[b, at, l * 128 + 512 : l * 128 + 640] = jnp.concatenate(ims, axis=0).astype(BF16)
        row = pl.multiple_of(((12 - b) % 12) * 32, 32)
        s_ref[...] += lax.dot_general(
            r2[pl.ds(row, 384), :], a_ref[b], (((1,), (1,)), ((), ())), preferred_element_type=F32
        )
        return carry

    lax.fori_loop(0, 12, one_block, 0)

    w128 = jnp.concatenate([w512] * 16, axis=0)
    pen = lax.dot_general(
        pw[...], w128, (((1,), (1,)), ((), ())), preferred_element_type=F32, precision=HIGHEST
    )
    mine = (
        lax.broadcasted_iota(jnp.int32, (KPAD, 100), 0) + c * 25
        == lax.broadcasted_iota(jnp.int32, (KPAD, 100), 1)
    )
    frac = jnp.sum(jnp.where(mine, frac_in[...], 0.0), axis=1, keepdims=True)
    base = jnp.log(jnp.where(frac > 0.0, frac, 1.0)) - 0.5 * pen
    base = jnp.concatenate([base, base], axis=1)
    away = lax.broadcasted_iota(jnp.int32, (16, 128), 0).astype(F32) - turn
    away = jnp.where(away < 0.0, away + 12.0, away)
    away = jnp.minimum(away, 12.0 - away)
    prior = -KAPPA * away * away
    prior = jnp.concatenate([prior, prior], axis=1)
    live = (lax.broadcasted_iota(jnp.int32, (KPAD, 256), 0) < 25) & (
        lax.broadcasted_iota(jnp.int32, (KPAD, 256), 1) < 200
    )
    top = jnp.full((KPAD, 256), -3e38, F32)
    for r in range(12):
        v = s_ref[r * 32 : r * 32 + 32, :] + (base + prior[r : r + 1, :])
        v = jnp.where(live, v, -3e38)
        s_ref[r * 32 : r * 32 + 32, :] = v
        top = jnp.maximum(top, v)
    here = fold(jnp.max(top, axis=0, keepdims=True), jnp.maximum)
    here256 = jnp.concatenate([here, here], axis=1)[0:1]
    total = jnp.zeros((KPAD, 256), F32)
    for r in range(12):
        v = jnp.where(live, jnp.exp(s_ref[r * 32 : r * 32 + 32, :] - here256), 0.0)
        s_ref[r * 32 : r * 32 + 32, :] = v
        total = total + v
    mass = fold(jnp.sum(total, axis=0, keepdims=True), jnp.add)
    sm_src[0:8] = here
    sm_src[8:16] = mass
    sm_copies = [remote(sm_src, sm.at[d], sm_s.at[d], sm_r.at[d], at_cls(d)) for d in range(1, 4)]
    for copy in sm_copies:
        copy.start()
    for copy in sm_copies:
        copy.wait()
    peak = here
    for d in range(1, 4):
        peak = jnp.maximum(peak, sm[d, 0:8])
    full = mass * jnp.exp(here - peak)
    for d in range(1, 4):
        full = full + sm[d, 8:16] * jnp.exp(sm[d, 0:8] - peak)
    evid = (peak + jnp.log(full))[0:1]
    first = jnp.sum(jnp.where(lane1 == 2 * c, evid, 0.0), axis=1, keepdims=True)
    second = jnp.sum(jnp.where(lane1 == 2 * c + 1, evid, 0.0), axis=1, keepdims=True)
    evid_ref[...] = jnp.where(lane1 == 0, first, second)[:, 0:2]
    scale = jnp.exp(here - peak) / full
    scale256 = jnp.concatenate([scale, scale], axis=1)[0:1]
    weight = jnp.zeros((KPAD, 256), F32)
    for r in range(12):
        v = s_ref[r * 32 : r * 32 + 32, :] * scale256
        weight = weight + v
        v = v.astype(BF16)
        j = (12 - r) % 12
        p2[j * 32 : j * 32 + 32, :] = v
        p2[(j + 12) * 32 : (j + 12) * 32 + 32, :] = v

    inv256 = jnp.concatenate([info] * 32, axis=0)
    dsrc[...] = lax.dot_general(
        weight, inv256, (((1,), (0,)), ((), ())), preferred_element_type=F32, precision=HIGHEST
    )
    dz_copies = [remote(dsrc, dz.at[d], dz_s.at[d], dz_r.at[d], at_z(d)) for d in range(1, 8)]
    for copy in dz_copies:
        copy.start()

    rs1_copies = []
    for i in range(4):
        offs = [pl.multiple_of(((h + 2 * i + 1 + e) % 8) * 128, 128) for e in range(2)]
        for b in range(12):
            rhs = jnp.concatenate([a_ref[b, :, pl.ds(o, 128)] for o in offs], axis=1)
            row = ((12 - b) % 12) * 32
            part = jnp.dot(p2[row : row + 384, :], rhs, preferred_element_type=F32)
            if b == 0:
                n_ref[...] = part
            else:
                n_ref[...] += part
        for e in range(2):
            for b in range(12):
                nb[pl.ds(e * ROWS + b, 25, stride=12), :] = n_ref[
                    b * 32 : b * 32 + 25, e * 128 : e * 128 + 128
                ]
            d = 2 * i + 1 + e
            if d < 8:
                encode(nb[e * ROWS : e * ROWS + ROWS, :], sb.at[d])
                copy = remote(sb.at[d], rs1.at[d], rs1_s.at[d], rs1_r.at[d], at_plane(d))
                copy.start()
                rs1_copies.append(copy)
            else:
                acc[...] = nb[e * ROWS : e * ROWS + ROWS, :]

    for copy in dz_copies:
        copy.wait()
    dsum = dsrc[...]
    for d in range(1, 8):
        dsum = dsum + dz[d]
    dpsrc[...] = dsum
    dp_copies = [remote(dpsrc, dp.at[d], dp_s.at[d], dp_r.at[d], at_plane(d)) for d in range(1, 8)]

    for copy in rs1_copies:
        copy.wait_recv()
    tot = acc[...]
    for d in range(1, 8):
        tot = tot + decode(rs1.at[d])
    ph2[0:ROWS, :] = tot
    rs2_copies = []
    for d in range(1, 8):
        at = pl.multiple_of(((z + d) % 8) * SLOT, 16)
        rs2_copies.append(
            remote(ph2.at[pl.ds(at, SLOT)], rs2.at[d], rs2_s.at[d], rs2_r.at[d], at_z(d))
        )
    for copy in rs2_copies:
        copy.start()
    for copy in dp_copies:
        copy.start()
    for copy in dp_copies:
        copy.wait()
    dsum = dpsrc[...]
    for d in range(1, 8):
        dsum = dsum + dp[d]
    square = (
        lax.broadcasted_iota(jnp.int32, (KPAD, KPAD), 0)
        == lax.broadcasted_iota(jnp.int32, (KPAD, KPAD), 1)
    )
    frac = jnp.sum(jnp.where(square, dsum[:, 32:33], 0.0), axis=0, keepdims=True)
    frac_ref[...] = frac[:, 0:25] * (1.0 / 512.0)
    rho = lax.broadcasted_iota(jnp.int32, (CYCLES, 128), 0)
    lane = lax.broadcasted_iota(jnp.int32, (CYCLES, 128), 1)
    pick = (rho == (h % 4) * 8 + lane // 16).astype(F32)
    mine = lax.broadcasted_iota(jnp.int32, (SLOT, KPAD), 0) // 12 + z * 4
    mine = (mine == lax.broadcasted_iota(jnp.int32, (SLOT, KPAD), 1)).astype(F32)
    div = jnp.dot(dsum[:, 0:CYCLES] + reg_ref[...], pick, preferred_element_type=F32, precision=HIGHEST)
    div = jnp.dot(mine, div, preferred_element_type=F32, precision=HIGHEST)
    own = pl.multiple_of(z * SLOT, 16)
    for copy in rs2_copies:
        copy.wait_recv()
    tot = ph2[pl.ds(own, SLOT), :]
    for d in range(1, 8):
        tot = tot + rs2[d]
    inside = lax.broadcasted_iota(jnp.int32, (SLOT, 128), 0) // 12 + z * 4 < 25
    tot = jnp.where(inside, tot / jnp.where(inside, div, 1.0), 0.0)

    loads[3].wait()
    loads[4].wait()
    high = tot.astype(BF16)
    low = (tot - high.astype(F32)).astype(BF16)
    wide = jnp.dot(jnp.concatenate([high, low], axis=0), spread_ref[...], preferred_element_type=F32)
    brow = lax.broadcasted_iota(jnp.int32, (SLOT, 128), 0) % 12
    slot = lax.broadcasted_iota(jnp.int32, (SLOT, 128), 1) // 16
    stack = jnp.concatenate(
        [
            jnp.concatenate(
                [
                    jnp.where(
                        slot == (4 * r + brow) % 8,
                        wide[i * SLOT : (i + 1) * SLOT, r * 128 : r * 128 + 128],
                        0.0,
                    )
                    for i in range(2)
                ],
                axis=1,
            )
            for r in range(8)
        ],
        axis=0,
    ).astype(BF16)
    both = jnp.dot(rows_ref[...], stack, preferred_element_type=F32)
    ag1[pl.ds(own, SLOT), :] = both[:, 0:128] + both[:, 128:256]
    ag1_copies = [
        remote(ag1.at[pl.ds(own, SLOT)], ag1.at[pl.ds(own, SLOT)], ag1_s.at[d], ag1_r.at[d], at_z(d))
        for d in range(1, 8)
    ]
    for copy in ag1_copies:
        copy.start()
    for copy in ag1_copies:
        copy.wait()
    encode(ag1[0:ROWS, :], ag2s)
    ag2_copies = [
        remote(ag2s, ag2.at[d], ag2_s.at[d], ag2_r.at[d], at_plane(d))
        for d in range(1, 8)
    ]
    for copy in ag2_copies:
        copy.start()

    def place(value, g):
        fin[...] = decode(value)
        for n in range(12):
            at = pl.multiple_of(g * 1536 + n * 128, 128)
            out_ref[:, pl.ds(at, 128)] = fin[pl.ds(n, 25, stride=12), :]

    place(ag2s, h)
    for d in range(1, 8):
        ag2_copies[d - 1].wait_recv()
        place(ag2.at[d], (h + 8 - d) % 8)
    for copy in ag2_copies + rs2_copies + rs1_copies:
        copy.wait_send()


def step(particles, references, centers, rot_prior, groups, class_frac, inv_noise, reg_inv):
    shift, center = tables()
    spread, rows = shard_maps()
    vmem = pl.BlockSpec(memory_space=pltpu.VMEM)
    dma = pltpu.SemaphoreType.DMA
    smem = pl.BlockSpec(memory_space=pltpu.SMEM)
    hbm = pl.BlockSpec(memory_space=pl.ANY)
    out, frac, evid = pl.pallas_call(
        kernel,
        out_shape=(
            jax.ShapeDtypeStruct((25, FEAT), F32),
            jax.ShapeDtypeStruct((1, 25), F32),
            jax.ShapeDtypeStruct((1, 2), F32),
        ),
        in_specs=[vmem] + [smem] * 3 + [vmem] * 3 + [hbm] * 5,
        out_specs=(vmem, vmem, vmem),
        scratch_shapes=[
            pltpu.VMEM((25, FEAT), BF16),
            pltpu.VMEM((12, 64, 512), F32),
            pltpu.VMEM((12, 16, 512), F32),
            pltpu.VMEM((128, 1024), BF16),
            pltpu.VMEM((SLOT, 8 * SLOT), BF16),
            pltpu.VMEM((16, 1536), F32),
            pltpu.VMEM((8, 128), F32),
            pltpu.VMEM((16, 1536), BF16),
            pltpu.VMEM((4, 16, 1536), BF16),
            pltpu.VMEM((4, 8, 128), F32),
            pltpu.VMEM((12 * 64, 128), F32),
            pltpu.VMEM((12, 8, 512), F32),
            pltpu.VMEM((12, 8, 512), F32),
            pltpu.VMEM((12, 256, 1024), BF16),
            pltpu.VMEM((24 * 32, 1024), BF16),
            pltpu.VMEM((KPAD, 512), F32),
            pltpu.VMEM((384, 256), F32),
            pltpu.VMEM((16, 128), F32),
            pltpu.VMEM((4, 16, 128), F32),
            pltpu.VMEM((24 * 32, 256), BF16),
            pltpu.VMEM((384, 256), F32),
            pltpu.VMEM((2 * ROWS, 128), F32),
            pltpu.VMEM((8, ROWS, 128), jnp.int16),
            pltpu.VMEM((8, ROWS, 128), jnp.int16),
            pltpu.VMEM((ROWS, 128), F32),
            pltpu.VMEM((8 * SLOT, 128), F32),
            pltpu.VMEM((8, SLOT, 128), F32),
            pltpu.VMEM((8 * SLOT, 128), F32),
            pltpu.VMEM((ROWS, 128), jnp.int16),
            pltpu.VMEM((8, ROWS, 128), jnp.int16),
            pltpu.VMEM((ROWS, 128), F32),
            pltpu.VMEM((KPAD, 128), F32),
            pltpu.VMEM((8, KPAD, 128), F32),
            pltpu.VMEM((KPAD, 128), F32),
            pltpu.VMEM((8, KPAD, 128), F32),
            dma((5,)),
        ]
        + [dma((4,))] * 6
        + [dma((8,))] * 12,
        compiler_params=pltpu.CompilerParams(
            collective_id=0, has_side_effects=True, vmem_limit_bytes=60 * 1024 * 1024
        ),
    )(
        particles, centers, rot_prior, groups, class_frac.reshape(1, 100), inv_noise,
        reg_inv.reshape(1, CYCLES), references, jnp.asarray(shift), jnp.asarray(center),
        jnp.asarray(spread, BF16), jnp.asarray(rows, BF16),
    )
    return out, frac.reshape(25), evid.reshape(2)


def solution(mesh):
    both = ("cls", "ptl")
    return jax.shard_map(
        step,
        mesh=mesh,
        in_specs=(P(both, None), P("cls", None), P(both, None), P(both), P(both), P(), P(), P()),
        out_specs=(P("cls", None), P("cls"), P(both)),
        check_vma=False,
    )
```

```python
import math

import jax
import jax.numpy as jnp
import numpy as np
from jax import lax
from jax.experimental import pallas as pl
from jax.experimental.pallas import tpu as pltpu
from jax.sharding import PartitionSpec as P

ROTS = 12
SPAN = 2
CYCLES = 32
ANGLES = 192
BOX = 128
SHIFTS = 25
FEAT = 12288
KAPPA = 0.25
HIGHEST = lax.Precision.HIGHEST
MESH = pl.DeviceIdType.MESH
F32, BF16 = jnp.float32, jnp.bfloat16

KPAD = 32
ROWS = 304
SLOT = 48


def tables():
    cycle = np.arange(CYCLES, dtype=np.float64) + 1.0
    angle = np.arange(ANGLES, dtype=np.float64) * (2.0 * math.pi / ANGLES)
    fx = cycle[:, None] * np.cos(angle)[None] / BOX
    fy = cycle[:, None] * np.sin(angle)[None] / BOX

    def blocked(v):
        n = v.shape[0]
        v = v.reshape(n, 4, 8, 12, 16)
        return np.transpose(v, (3, 0, 1, 2, 4)).reshape(12, n, 512)

    t = np.arange(SHIFTS)
    mx, my = t // 5 - SPAN, t % 5 - SPAN
    ph = 2.0 * math.pi * (mx[:, None, None] * fx + my[:, None, None] * fy)
    shift = np.concatenate([np.cos(ph), np.zeros((7, 32, 192)), np.sin(ph), np.zeros((7, 32, 192))])
    rows = []
    for f in (fx, fy):
        for m in (1, 2, 3):
            rows += [np.cos(2.0 * math.pi * m * f), np.sin(2.0 * math.pi * m * f)]
    center = np.stack(rows + [np.zeros_like(fx)] * 4)
    return blocked(shift).astype(np.float32), blocked(center).astype(np.float32)


def shard_maps():
    spread = np.zeros((128, 1024), np.float32)
    for rho in range(8):
        for j in range(8):
            for s in range(16):
                spread[rho * 16 + s, rho * 128 + j * 16 + s] = 1
    rows = np.zeros((SLOT, 8 * SLOT), np.float32)
    for rho in range(8):
        for k in range(4):
            for b in range(12):
                rows[k * 12 + (12 * rho + b) // 8, rho * SLOT + k * 12 + b] = 1
    return spread, rows


def to_blocks(nat):
    lane = lax.broadcasted_iota(jnp.int32, nat[0].shape, 1) // 16
    out = []
    for b in range(12):
        acc = None
        for rho in range(8):
            n, j = divmod(12 * rho + b, 8)
            v = nat[n] if j == rho else pltpu.roll(nat[n], (16 * (rho - j)) % 128, 1)
            acc = v if acc is None else jnp.where(lane == rho, v, acc)
        out.append(acc)
    return out


def fold(v, op):
    v = jnp.broadcast_to(op(v[:, :128], v[:, 128:]), (8, 128))
    for step in (8, 16, 32, 64):
        v = op(v, pltpu.roll(v, step, 1))
    return v


def encode(value, to):
    top = jnp.max(jnp.abs(value), axis=0, keepdims=True)
    power = jnp.ceil(jnp.log2(jnp.maximum(top, 1e-30)) + 1e-3) - 15.0
    code = jnp.round(value * jnp.exp2(-power))
    row = lax.broadcasted_iota(jnp.int32, value.shape, 0)
    to[...] = jnp.where(row == 300, power, code).astype(jnp.int32).astype(jnp.int16)


def decode(code):
    value = code[...].astype(jnp.int32).astype(F32)
    return value * jnp.exp2(value[300:301])


def encode_rows(value):
    top = jnp.max(jnp.abs(value), axis=0, keepdims=True)
    power = jnp.ceil(jnp.log2(jnp.maximum(top, 1e-30)) + 1e-3) - 15.0
    code = jnp.round(value * jnp.exp2(-power)).astype(jnp.int32).astype(jnp.int16)
    return code, power


def kernel(
    x_hbm, cen_hbm, rot_hbm, group_hbm, frac_hbm, noise_hbm, reg_hbm,
    refs_hbm, shift_hbm, center_hbm, spread_hbm, rows_hbm,
    gc, ge, frac_ref, evid_ref,
    x_ref, cen_ref, rot_ref, group_ref, frac_in, noise_ref, reg_ref,
    refs_ref, shift_ref, center_ref, spread_ref, rows_ref,
    xs, ms, xb, xg, mg, xf, yre, yim, a_ref, r2, pw, s_ref, sm_src, sm, p2, n_ref, nb, sb, rs1, acc,
    ph2, ph2c, ph2e, rs2, rs2e, agc, age, fin, dsrc, dz, dpsrc, dp, in_s,
    x_s, x_r, m_s, m_r, sm_s, sm_r, rs1_s, rs1_r, rs2_s, rs2_r, ag1_s, ag1_r, ag2_s, ag2_r, re_s, re_r, ae_s, ae_r, ge_s, ge_r,
    dz_s, dz_r, dp_s, dp_r,
):
    c = lax.axis_index("cls")
    q = lax.axis_index("ptl")
    h, z = q // 8, q % 8

    def at_cls(d):
        return ((c + d) % 4, q)

    def at_z(d):
        return (c, h * 8 + (z + d) % 8)

    def at_plane(d):
        return (c, ((h + d) % 8) * 8 + z)

    loads = [
        pltpu.make_async_copy(src, dst, in_s.at[i])
        for i, (src, dst) in enumerate(
            (
                (refs_hbm, refs_ref), (center_hbm, center_ref), (shift_hbm, shift_ref),
                (spread_hbm, spread_ref), (rows_hbm, rows_ref),
                (frac_hbm, frac_in), (reg_hbm, reg_ref),
                (cen_hbm, cen_ref), (rot_hbm, rot_ref), (group_hbm, group_ref),
                (noise_hbm, noise_ref), (x_hbm, x_ref),
            )
        )
    ]
    for load in loads[::-1]:
        load.start()
    barrier = pltpu.get_barrier_semaphore()
    for d in range(1, 4):
        pl.semaphore_signal(barrier, inc=1, device_id=at_cls(d), device_id_type=MESH)
    for d in range(1, 8):
        pl.semaphore_signal(barrier, inc=1, device_id=at_z(d), device_id_type=MESH)
        pl.semaphore_signal(barrier, inc=1, device_id=at_plane(d), device_id_type=MESH)

    lane1 = lax.broadcasted_iota(jnp.int32, (1, 128), 1)
    ms[...] = jnp.zeros_like(ms)
    for load in loads[7:]:
        load.wait()
    for p in range(2):
        for g in range(8):
            xs[p * 8 + g : p * 8 + g + 1, :] = x_ref[p : p + 1, g * 1536 : (g + 1) * 1536].astype(F32)
        group = lax.broadcasted_iota(jnp.int32, (16, CYCLES), 0) == group_ref[p]
        inv = jnp.sum(jnp.where(group, noise_ref[...], 0.0), axis=0, keepdims=True)
        info = jnp.concatenate([inv, jnp.ones((1, 96), F32)], axis=1)
        for at, value in ((40, cen_ref[p, 0]), (41, cen_ref[p, 1]), (42, rot_ref[p])):
            info = jnp.where(lane1 == at, value.astype(F32), info)
        ms[p * 4 : p * 4 + 1, :] = info
    xb[...] = xs[...].astype(BF16)
    xg[c] = xb[...]
    mg[c] = ms[...]

    def remote(src, dst, ss, rs, dev):
        return pltpu.make_async_remote_copy(
            src_ref=src, dst_ref=dst, send_sem=ss, recv_sem=rs, device_id=dev, device_id_type=MESH
        )

    pw[...] = jnp.zeros_like(pw)
    loads[0].wait()

    def one_group(g, carry):
        at = pl.multiple_of(g * 1536, 1536)
        nat = [refs_ref[:, pl.ds(at + n * 128, 128)].astype(F32) for n in range(12)]
        blocks = to_blocks(nat)
        power = blocks[0] * blocks[0]
        for b in range(1, 12):
            power = power + blocks[b] * blocks[b]
        to = pl.multiple_of(g * 128, 128)
        pw[0:25, pl.ds(pl.multiple_of((g % 4) * 128, 128), 128)] += power
        for b in range(12):
            v = blocks[b].astype(BF16)
            j = (12 - b) % 12
            r2[j * 32 : j * 32 + 25, pl.ds(to, 128)] = v
            r2[(j + 12) * 32 : (j + 12) * 32 + 25, pl.ds(to, 128)] = v
        return carry

    lax.fori_loop(0, 8, one_group, 0)
    for b in range(12):
        a_ref[b * 256 + 192 : b * 256 + 256, :] = jnp.zeros((64, 1024), BF16)
    s_ref[...] = jnp.zeros_like(s_ref)
    nb[...] = jnp.zeros_like(nb)
    ph2[...] = jnp.zeros_like(ph2)
    pl.semaphore_wait(barrier, 17)

    x_copies = []
    for d in range(1, 4):
        x_copies.append(remote(ms, mg.at[c], m_s.at[d], m_r.at[d], at_cls(d)))
        x_copies.append(remote(xb, xg.at[c], x_s.at[d], x_r.at[d], at_cls(d)))
    for copy in x_copies:
        copy.start()


    for load in loads[1:7]:
        load.wait()
    for copy in x_copies:
        copy.wait()

    for i in range(4):
        for n in range(12):
            at = n * 64 + i * 16
            xf[at : at + 16, :] = xg[i, :, n * 128 : n * 128 + 128].astype(F32)
    for i in range(4):
        fin[i * 8 : i * 8 + 8, :] = mg[i]
    info = fin[pl.ds(0, 8, stride=4), :]
    lane8 = lax.broadcasted_iota(jnp.int32, (8, 128), 1)
    cx, cy = info[:, 40:41], info[:, 41:42]
    turn = jnp.where(lane8 % 8 == lax.broadcasted_iota(jnp.int32, (8, 128), 0), info[:, 42:43], 0.0)
    turn = jnp.sum(turn, axis=0, keepdims=True)
    grow = (
        lax.broadcasted_iota(jnp.int32, (CYCLES, 512), 0)
        == lax.broadcasted_iota(jnp.int32, (CYCLES, 512), 1) // 16
    ).astype(F32)
    w512 = jnp.dot(info[:, 0:CYCLES], grow, preferred_element_type=F32, precision=HIGHEST)
    w = [w512[:, i * 128 : i * 128 + 128] for i in range(4)]

    def phase(value, row, b, gq):
        size = jnp.abs(value)
        cos, sin = jnp.ones((8, 128), F32), jnp.zeros((8, 128), F32)
        for m in (1, 2, 3):
            hit = size == float(m)
            at = row + (m - 1) * 2
            cos = jnp.where(hit, center_ref[b, at : at + 1, gq * 128 : gq * 128 + 128], cos)
            sin = jnp.where(hit, center_ref[b, at + 1 : at + 2, gq * 128 : gq * 128 + 128], sin)
        return cos, jnp.where(value < 0.0, -sin, sin)

    for gq in range(4):
        re = to_blocks([xf[pl.ds(n * 64 + gq, 8, stride=8), :] for n in range(12)])
        im = to_blocks([xf[pl.ds(n * 64 + gq + 4, 8, stride=8), :] for n in range(12)])
        for b in range(12):
            xc, xs = phase(cx, 0, b, gq)
            yc, ys = phase(cy, 6, b, gq)
            pc, ps = xc * yc - xs * ys, xc * ys + xs * yc
            u, v = re[b] * w[gq], im[b] * w[gq]
            yre[b, :, gq * 128 : gq * 128 + 128] = u * pc - v * ps
            yim[b, :, gq * 128 : gq * 128 + 128] = u * ps + v * pc

    def one_block(b, carry):
        for l in range(4):
            cols = slice(l * 128, l * 128 + 128)
            u, v = yre[b, :, cols], yim[b, :, cols]
            for t in range(0, 25, 2):
                res, ims = [], []
                for tt in range(t, min(t + 2, 25)):
                    tc = shift_ref[b, tt : tt + 1, cols]
                    ts = shift_ref[b, 32 + tt : 33 + tt, cols]
                    res.append(u * tc - v * ts)
                    ims.append(u * ts + v * tc)
                if len(res) == 1:
                    res.append(jnp.zeros((8, 128), F32))
                    ims.append(jnp.zeros((8, 128), F32))
                at = pl.ds(pl.multiple_of(b * 256 + t * 8, 16), 16)
                a_ref[at, cols] = jnp.concatenate(res, axis=0).astype(BF16)
                a_ref[at, l * 128 + 512 : l * 128 + 640] = jnp.concatenate(ims, axis=0).astype(BF16)
        row = pl.multiple_of(((12 - b) % 12) * 32, 32)
        s_ref[...] += lax.dot_general(
            r2[pl.ds(row, 384), :],
            a_ref[pl.ds(pl.multiple_of(b * 256, 256), 256), :],
            (((1,), (1,)), ((), ())), preferred_element_type=F32
        )
        return carry

    lax.fori_loop(0, 12, one_block, 0)

    w128 = jnp.concatenate([w512] * 16, axis=0)
    pen = lax.dot_general(
        pw[...], w128, (((1,), (1,)), ((), ())), preferred_element_type=F32, precision=HIGHEST
    )
    mine = (
        lax.broadcasted_iota(jnp.int32, (KPAD, 100), 0) + c * 25
        == lax.broadcasted_iota(jnp.int32, (KPAD, 100), 1)
    )
    frac = jnp.sum(jnp.where(mine, frac_in[...], 0.0), axis=1, keepdims=True)
    base = jnp.log(jnp.where(frac > 0.0, frac, 1.0)) - 0.5 * pen
    base = jnp.concatenate([base, base], axis=1)
    away = lax.broadcasted_iota(jnp.int32, (16, 128), 0).astype(F32) - turn
    away = jnp.where(away < 0.0, away + 12.0, away)
    away = jnp.minimum(away, 12.0 - away)
    prior = -KAPPA * away * away
    prior = jnp.concatenate([prior, prior], axis=1)
    live = (lax.broadcasted_iota(jnp.int32, (KPAD, 256), 0) < 25) & (
        lax.broadcasted_iota(jnp.int32, (KPAD, 256), 1) < 200
    )
    top = jnp.full((KPAD, 256), -3e38, F32)
    for r in range(12):
        v = s_ref[r * 32 : r * 32 + 32, :] + (base + prior[r : r + 1, :])
        v = jnp.where(live, v, -3e38)
        s_ref[r * 32 : r * 32 + 32, :] = v
        top = jnp.maximum(top, v)
    here = fold(jnp.max(top, axis=0, keepdims=True), jnp.maximum)
    here256 = jnp.concatenate([here, here], axis=1)[0:1]
    total = jnp.zeros((KPAD, 256), F32)
    for r in range(12):
        v = jnp.where(live, jnp.exp(s_ref[r * 32 : r * 32 + 32, :] - here256), 0.0)
        s_ref[r * 32 : r * 32 + 32, :] = v
        total = total + v
    mass = fold(jnp.sum(total, axis=0, keepdims=True), jnp.add)
    sm_src[0:8] = here
    sm_src[8:16] = mass
    sm_copies = [remote(sm_src, sm.at[d], sm_s.at[d], sm_r.at[d], at_cls(d)) for d in range(1, 4)]
    for copy in sm_copies:
        copy.start()
    for copy in sm_copies:
        copy.wait()
    peak = here
    for d in range(1, 4):
        peak = jnp.maximum(peak, sm[d, 0:8])
    full = mass * jnp.exp(here - peak)
    for d in range(1, 4):
        full = full + sm[d, 8:16] * jnp.exp(sm[d, 0:8] - peak)
    evid = (peak + jnp.log(full))[0:1]
    first = jnp.sum(jnp.where(lane1 == 2 * c, evid, 0.0), axis=1, keepdims=True)
    second = jnp.sum(jnp.where(lane1 == 2 * c + 1, evid, 0.0), axis=1, keepdims=True)
    evid_ref[...] = jnp.where(lane1 == 0, first, second)[:, 0:2]
    scale = jnp.exp(here - peak) / full
    scale256 = jnp.concatenate([scale, scale], axis=1)[0:1]
    weight = jnp.zeros((KPAD, 256), F32)
    for r in range(12):
        v = s_ref[r * 32 : r * 32 + 32, :] * scale256
        weight = weight + v
        v = v.astype(BF16)
        for b1 in range(12):
            b = (b1 - r) % 12
            p2[b * 32 : b * 32 + 32, b1 * 256 : b1 * 256 + 256] = v

    inv256 = jnp.concatenate([info] * 32, axis=0)
    dsrc[...] = lax.dot_general(
        weight, inv256, (((1,), (0,)), ((), ())), preferred_element_type=F32, precision=HIGHEST
    )
    dz_copies = [remote(dsrc, dz.at[d], dz_s.at[d], dz_r.at[d], at_z(d)) for d in range(1, 8)]
    for copy in dz_copies:
        copy.start()

    def weighted(d, width):
        offs = [pl.multiple_of(((h + d + e) % 8) * 128, 128) for e in range(width)]
        rhs = jnp.concatenate([a_ref[:, pl.ds(o, 128)] for o in offs], axis=1)
        n_ref[...] = jnp.dot(p2[...], rhs, preferred_element_type=F32)
        for e in range(2):
            for b in range(12):
                nb[pl.ds(e * ROWS + b, 25, stride=12), :] = n_ref[
                    b * 32 : b * 32 + 25, e * 128 : e * 128 + 128
                ]

    def rs1_copy(d):
        return remote(sb.at[d], rs1.at[d], rs1_s.at[d], rs1_r.at[d], at_plane(d))

    def send_sum(d, e):
        encode(nb[e * ROWS : e * ROWS + ROWS, :], sb.at[d])
        rs1_copy(d).start()

    def one_pair(i, carry):
        weighted(2 * i + 1, 2)
        send_sum(2 * i + 1, 0)
        send_sum(2 * i + 2, 1)
        return carry

    lax.fori_loop(0, 3, one_pair, 0)
    weighted(7, 2)
    send_sum(7, 0)
    acc[...] = nb[ROWS : 2 * ROWS, :]
    rs1_copies = [rs1_copy(d) for d in range(1, 8)]

    for copy in dz_copies:
        copy.wait()
    dsum = dsrc[...]
    for d in range(1, 8):
        dsum = dsum + dz[d]
    dpsrc[...] = dsum
    dp_copies = [remote(dpsrc, dp.at[d], dp_s.at[d], dp_r.at[d], at_plane(d)) for d in range(1, 8)]
    for copy in dp_copies:
        copy.start()

    tot = acc[...]
    for d in range(1, 8):
        rs1_copies[d - 1].wait_recv()
        tot = tot + decode(rs1.at[d])
    tot = jnp.where(lax.broadcasted_iota(jnp.int32, (ROWS, 128), 0) < 300, tot, 0.0)
    ph2[0:ROWS, :] = tot
    code, power = encode_rows(tot)
    ph2c[0:ROWS, :] = code
    ph2e[...] = power

    def sized(zs, make, act):
        @pl.when(zs < 6)
        def _():
            act(make(SLOT))

        @pl.when(zs == 6)
        def _():
            act(make(16))

    def rs2_copy(d):
        def make(size):
            at = pl.multiple_of(((z + d) % 8) * SLOT, 16)
            return remote(
                ph2c.at[pl.ds(at, size)], rs2.at[d, pl.ds(0, size)], rs2_s.at[d], rs2_r.at[d], at_z(d)
            )

        return make

    re_copies = [remote(ph2e, rs2e.at[d], re_s.at[d], re_r.at[d], at_z(d)) for d in range(1, 8)]
    for d in range(1, 8):
        sized((z + d) % 8, rs2_copy(d), lambda copy: copy.start())
        re_copies[d - 1].start()
    for copy in dp_copies:
        copy.wait()
    dsum = dpsrc[...]
    for d in range(1, 8):
        dsum = dsum + dp[d]
    square = (
        lax.broadcasted_iota(jnp.int32, (KPAD, KPAD), 0)
        == lax.broadcasted_iota(jnp.int32, (KPAD, KPAD), 1)
    )
    frac = jnp.sum(jnp.where(square, dsum[:, 32:33], 0.0), axis=0, keepdims=True)
    frac_ref[...] = frac[:, 0:25] * (1.0 / 512.0)
    rho = lax.broadcasted_iota(jnp.int32, (CYCLES, 128), 0)
    lane = lax.broadcasted_iota(jnp.int32, (CYCLES, 128), 1)
    pick = (rho == (h % 4) * 8 + lane // 16).astype(F32)
    mine = lax.broadcasted_iota(jnp.int32, (SLOT, KPAD), 0) // 12 + z * 4
    mine = (mine == lax.broadcasted_iota(jnp.int32, (SLOT, KPAD), 1)).astype(F32)
    div = jnp.dot(dsum[:, 0:CYCLES] + reg_ref[...], pick, preferred_element_type=F32, precision=HIGHEST)
    div = jnp.dot(mine, div, preferred_element_type=F32, precision=HIGHEST)
    own = pl.multiple_of(z * SLOT, 16)
    tot = ph2[pl.ds(own, SLOT), :]
    for d in range(1, 8):
        sized(z, rs2_copy(d), lambda copy: copy.wait_recv())
        re_copies[d - 1].wait_recv()
        tot = tot + rs2[d].astype(jnp.int32).astype(F32) * jnp.exp2(rs2e[d])
    inside = lax.broadcasted_iota(jnp.int32, (SLOT, 128), 0) // 12 + z * 4 < 25
    tot = jnp.where(inside, tot / jnp.where(inside, div, 1.0), 0.0)

    high = tot.astype(BF16)
    low = (tot - high.astype(F32)).astype(BF16)
    wide = jnp.dot(jnp.concatenate([high, low], axis=0), spread_ref[...], preferred_element_type=F32)
    brow = lax.broadcasted_iota(jnp.int32, (SLOT, 128), 0) % 12
    slot = lax.broadcasted_iota(jnp.int32, (SLOT, 128), 1) // 16
    stack = jnp.concatenate(
        [
            jnp.concatenate(
                [
                    jnp.where(
                        slot == (4 * r + brow) % 8,
                        wide[i * SLOT : (i + 1) * SLOT, r * 128 : r * 128 + 128],
                        0.0,
                    )
                    for i in range(2)
                ],
                axis=1,
            )
            for r in range(8)
        ],
        axis=0,
    ).astype(BF16)
    both = jnp.dot(rows_ref[...], stack, preferred_element_type=F32)
    code, power = encode_rows(both[:, 0:128] + both[:, 128:256])
    agc[z] = code
    age[z] = power

    def ag1_copy(d):
        def make(size):
            mine = agc.at[z, pl.ds(0, size)]
            return remote(mine, mine, ag1_s.at[d], ag1_r.at[d], at_z(d))

        return make

    def ag2_copy(dz_, d):
        def make(size):
            zs = (z + 8 - dz_) % 8
            return remote(
                agc.at[zs, pl.ds(0, size)],
                gc.at[h, zs, pl.ds(0, size)],
                ag2_s.at[dz_, d],
                ag2_r.at[dz_, d],
                at_plane(d),
            )

        return make

    ae_copies = [remote(age.at[z], age.at[z], ae_s.at[d], ae_r.at[d], at_z(d)) for d in range(1, 8)]
    ge_copies = [remote(age, ge.at[h], ge_s.at[d], ge_r.at[d], at_plane(d)) for d in range(1, 8)]
    for d in range(1, 8):
        sized(z, ag1_copy(d), lambda copy: copy.start())
        ae_copies[d - 1].start()
    for d in range(1, 8):
        sized(z, ag2_copy(0, d), lambda copy: copy.start())
    for dz_ in range(1, 8):
        zs = (z + 8 - dz_) % 8
        sized(zs, ag1_copy(dz_), lambda copy: copy.wait_recv())
        for d in range(1, 8):
            sized(zs, ag2_copy(dz_, d), lambda copy: copy.start())
        ae_copies[dz_ - 1].wait_recv()
    for copy in ge_copies:
        copy.start()

    own_copies = [
        pltpu.make_async_copy(agc, gc.at[h], in_s.at[12]),
        pltpu.make_async_copy(age, ge.at[h], in_s.at[13]),
    ]
    for copy in own_copies:
        copy.start()
    for d in range(1, 8):
        for dz_ in range(8):
            sized((z + 8 - dz_) % 8, ag2_copy(dz_, d), lambda copy: copy.wait_recv())
        ge_copies[d - 1].wait_recv()
    for copy in own_copies:
        copy.wait()
    for d in range(1, 8):
        sized((z + d) % 8, rs2_copy(d), lambda copy: copy.wait_send())
        sized(z, ag1_copy(d), lambda copy: copy.wait_send())
        for dz_ in range(8):
            sized((z + 8 - dz_) % 8, ag2_copy(dz_, d), lambda copy: copy.wait_send())
    for copy in rs1_copies + re_copies + ae_copies + ge_copies:
        copy.wait_send()


def finish(code_ref, power_ref, frac_in, evid_in, out_ref, frac_ref, evid_ref, fin):
    for g in range(4):
        for zs in range(7):
            code = code_ref[g, zs].astype(jnp.int32).astype(F32)
            fin[zs * SLOT : (zs + 1) * SLOT, :] = code * jnp.exp2(power_ref[g, zs])
        for n in range(12):
            at = g * 1536 + n * 128
            out_ref[:, at : at + 128] = fin[pl.ds(n, 25, stride=12), :]
    frac_ref[...] = frac_in[...]
    evid_ref[...] = evid_in[...]


def step(particles, references, centers, rot_prior, groups, class_frac, inv_noise, reg_inv):
    shift, center = tables()
    spread, rows = shard_maps()
    vmem = pl.BlockSpec(memory_space=pltpu.VMEM)
    dma = pltpu.SemaphoreType.DMA
    hbm = pl.BlockSpec(memory_space=pltpu.HBM)
    code, power, frac, evid = pl.pallas_call(
        kernel,
        out_shape=(
            jax.ShapeDtypeStruct((8, 8, SLOT, 128), jnp.int16),
            jax.ShapeDtypeStruct((8, 8, 1, 128), F32),
            jax.ShapeDtypeStruct((1, 25), F32),
            jax.ShapeDtypeStruct((1, 2), F32),
        ),
        in_specs=[hbm] * 12,
        out_specs=(hbm, hbm, vmem, vmem),
        scratch_shapes=[
            pltpu.VMEM((2, FEAT), BF16),
            pltpu.SMEM((2, 2), jnp.int32),
            pltpu.SMEM((2,), jnp.int32),
            pltpu.SMEM((2,), jnp.int32),
            pltpu.VMEM((1, 100), F32),
            pltpu.VMEM((16, CYCLES), F32),
            pltpu.VMEM((1, CYCLES), F32),
            pltpu.VMEM((25, FEAT), BF16),
            pltpu.VMEM((12, 64, 512), F32),
            pltpu.VMEM((12, 16, 512), F32),
            pltpu.VMEM((128, 1024), BF16),
            pltpu.VMEM((SLOT, 8 * SLOT), BF16),
            pltpu.VMEM((16, 1536), F32),
            pltpu.VMEM((8, 128), F32),
            pltpu.VMEM((16, 1536), BF16),
            pltpu.VMEM((4, 16, 1536), BF16),
            pltpu.VMEM((4, 8, 128), F32),
            pltpu.VMEM((12 * 64, 128), F32),
            pltpu.VMEM((12, 8, 512), F32),
            pltpu.VMEM((12, 8, 512), F32),
            pltpu.VMEM((12 * 256, 1024), BF16),
            pltpu.VMEM((24 * 32, 1024), BF16),
            pltpu.VMEM((KPAD, 512), F32),
            pltpu.VMEM((384, 256), F32),
            pltpu.VMEM((16, 128), F32),
            pltpu.VMEM((4, 16, 128), F32),
            pltpu.VMEM((384, 12 * 256), BF16),
            pltpu.VMEM((384, 256), F32),
            pltpu.VMEM((2 * ROWS, 128), F32),
            pltpu.VMEM((8, ROWS, 128), jnp.int16),
            pltpu.VMEM((8, ROWS, 128), jnp.int16),
            pltpu.VMEM((ROWS, 128), F32),
            pltpu.VMEM((8 * SLOT, 128), F32),
            pltpu.VMEM((8 * SLOT, 128), jnp.int16),
            pltpu.VMEM((1, 128), F32),
            pltpu.VMEM((8, SLOT, 128), jnp.int16),
            pltpu.VMEM((8, 1, 128), F32),
            pltpu.VMEM((8, SLOT, 128), jnp.int16),
            pltpu.VMEM((8, 1, 128), F32),
            pltpu.VMEM((KPAD, 128), F32),
            pltpu.VMEM((KPAD, 128), F32),
            pltpu.VMEM((8, KPAD, 128), F32),
            pltpu.VMEM((KPAD, 128), F32),
            pltpu.VMEM((8, KPAD, 128), F32),
            dma((14,)),
        ]
        + [dma((4,))] * 6
        + [dma((8,))] * 6
        + [dma((8, 8))] * 2
        + [dma((8,))] * 10,
        compiler_params=pltpu.CompilerParams(
            collective_id=0, has_side_effects=True, vmem_limit_bytes=60 * 1024 * 1024
        ),
    )(
        particles, centers, rot_prior, groups, class_frac.reshape(1, 100), inv_noise,
        reg_inv.reshape(1, CYCLES), references, jnp.asarray(shift), jnp.asarray(center),
        jnp.asarray(spread, BF16), jnp.asarray(rows, BF16),
    )
    one = lambda shape: pl.BlockSpec(shape, lambda g: (0,) * len(shape))
    out, frac, evid = pl.pallas_call(
        finish,
        grid=(2,),
        out_shape=(
            jax.ShapeDtypeStruct((25, FEAT), F32),
            jax.ShapeDtypeStruct((1, 25), F32),
            jax.ShapeDtypeStruct((1, 2), F32),
        ),
        in_specs=[
            pl.BlockSpec((4, 8, SLOT, 128), lambda g: (g, 0, 0, 0)),
            pl.BlockSpec((4, 8, 1, 128), lambda g: (g, 0, 0, 0)),
            one((1, 25)),
            one((1, 2)),
        ],
        out_specs=(pl.BlockSpec((25, 6144), lambda g: (0, g)), one((1, 25)), one((1, 2))),
        scratch_shapes=[pltpu.VMEM((8 * SLOT, 128), F32)],
        compiler_params=pltpu.CompilerParams(vmem_limit_bytes=60 * 1024 * 1024),
    )(code, power, frac, evid)
    return out, frac.reshape(25), evid.reshape(2)


def solution(mesh):
    both = ("cls", "ptl")
    return jax.shard_map(
        step,
        mesh=mesh,
        in_specs=(P(both, None), P("cls", None), P(both, None), P(both), P(both), P(), P(), P()),
        out_specs=(P("cls", None), P("cls"), P(both)),
        check_vma=False,
    )
```

```python
import math

import jax
import jax.numpy as jnp
import numpy as np
from jax import lax
from jax.experimental import pallas as pl
from jax.experimental.pallas import tpu as pltpu
from jax.sharding import PartitionSpec as P

ROTS = 12
SPAN = 2
CYCLES = 32
ANGLES = 192
BOX = 128
SHIFTS = 25
FEAT = 12288
KAPPA = 0.25
HIGHEST = lax.Precision.HIGHEST
MESH = pl.DeviceIdType.MESH
F32, BF16 = jnp.float32, jnp.bfloat16

KPAD = 32
ROWS = 304
SLOT = 48


def tables():
    cycle = np.arange(CYCLES, dtype=np.float64) + 1.0
    angle = np.arange(ANGLES, dtype=np.float64) * (2.0 * math.pi / ANGLES)
    fx = cycle[:, None] * np.cos(angle)[None] / BOX
    fy = cycle[:, None] * np.sin(angle)[None] / BOX

    def blocked(v):
        n = v.shape[0]
        v = v.reshape(n, 4, 8, 12, 16)
        return np.transpose(v, (3, 0, 1, 2, 4)).reshape(12, n, 512)

    t = np.arange(SHIFTS)
    mx, my = t // 5 - SPAN, t % 5 - SPAN
    ph = 2.0 * math.pi * (mx[:, None, None] * fx + my[:, None, None] * fy)
    shift = np.concatenate([np.cos(ph), np.zeros((7, 32, 192)), np.sin(ph), np.zeros((7, 32, 192))])
    rows = []
    for f in (fx, fy):
        for m in (1, 2, 3):
            rows += [np.cos(2.0 * math.pi * m * f), np.sin(2.0 * math.pi * m * f)]
    center = np.stack(rows + [np.zeros_like(fx)] * 4)
    return blocked(shift).astype(np.float32), blocked(center).astype(np.float32)


def shard_maps():
    spread = np.zeros((128, 1024), np.float32)
    for rho in range(8):
        for j in range(8):
            for s in range(16):
                spread[rho * 16 + s, rho * 128 + j * 16 + s] = 1
    rows = np.zeros((SLOT, 8 * SLOT), np.float32)
    for rho in range(8):
        for k in range(4):
            for b in range(12):
                rows[k * 12 + (12 * rho + b) // 8, rho * SLOT + k * 12 + b] = 1
    return spread, rows


def to_blocks(nat):
    lane = lax.broadcasted_iota(jnp.int32, nat[0].shape, 1) // 16
    out = []
    for b in range(12):
        acc = None
        for rho in range(8):
            n, j = divmod(12 * rho + b, 8)
            v = nat[n] if j == rho else pltpu.roll(nat[n], (16 * (rho - j)) % 128, 1)
            acc = v if acc is None else jnp.where(lane == rho, v, acc)
        out.append(acc)
    return out


def fold(v, op):
    v = jnp.broadcast_to(op(v[:, :128], v[:, 128:]), (8, 128))
    for step in (8, 16, 32, 64):
        v = op(v, pltpu.roll(v, step, 1))
    return v


def encode(value, to):
    top = jnp.max(jnp.abs(value), axis=0, keepdims=True)
    power = jnp.ceil(jnp.log2(jnp.maximum(top, 1e-30)) + 1e-3) - 15.0
    code = jnp.round(value * jnp.exp2(-power))
    row = lax.broadcasted_iota(jnp.int32, value.shape, 0)
    to[...] = jnp.where(row == 300, power, code).astype(jnp.int32).astype(jnp.int16)


def decode(code):
    value = code[...].astype(jnp.int32).astype(F32)
    return value * jnp.exp2(value[300:301])


def encode_rows(value):
    top = jnp.max(jnp.abs(value), axis=0, keepdims=True)
    power = jnp.ceil(jnp.log2(jnp.maximum(top, 1e-30)) + 1e-3) - 15.0
    code = jnp.round(value * jnp.exp2(-power)).astype(jnp.int32).astype(jnp.int16)
    return code, power


def kernel(
    x_hbm, cen_hbm, rot_hbm, group_hbm, frac_hbm, noise_hbm, reg_hbm,
    refs_hbm, shift_hbm, center_hbm, spread_hbm, rows_hbm,
    gc, ge, frac_ref, evid_ref,
    x_ref, cen_ref, rot_ref, group_ref, frac_in, noise_ref, reg_ref,
    refs_ref, shift_ref, center_ref, spread_ref, rows_ref,
    xs, ms, xb, xg, mg, xf, yre, yim, a_ref, r2, pw, s_ref, sm_src, sm, p2, n_ref, nb, sb, rs1, acc,
    ph2, ph2c, ph2e, rs2, rs2e, agc, age, fin, dsrc, dz, dpsrc, dp, in_s,
    x_s, x_r, m_s, m_r, sm_s, sm_r, rs1_s, rs1_r, rs2_s, rs2_r, ag1_s, ag1_r, ag2_s, ag2_r, re_s, re_r, ae_s, ae_r, ge_s, ge_r,
    dz_s, dz_r, dp_s, dp_r,
):
    c = lax.axis_index("cls")
    q = lax.axis_index("ptl")
    h, z = q // 8, q % 8

    def at_cls(d):
        return ((c + d) % 4, q)

    def at_z(d):
        return (c, h * 8 + (z + d) % 8)

    def at_plane(d):
        return (c, ((h + d) % 8) * 8 + z)

    loads = [
        pltpu.make_async_copy(src, dst, in_s.at[i])
        for i, (src, dst) in enumerate(
            (
                (refs_hbm, refs_ref), (center_hbm, center_ref), (shift_hbm, shift_ref),
                (spread_hbm, spread_ref), (rows_hbm, rows_ref),
                (frac_hbm, frac_in), (reg_hbm, reg_ref),
                (cen_hbm, cen_ref), (rot_hbm, rot_ref), (group_hbm, group_ref),
                (noise_hbm, noise_ref), (x_hbm, x_ref),
            )
        )
    ]
    for load in loads[::-1]:
        load.start()
    barrier = pltpu.get_barrier_semaphore()
    for d in range(1, 4):
        pl.semaphore_signal(barrier, inc=1, device_id=at_cls(d), device_id_type=MESH)
    for d in range(1, 8):
        pl.semaphore_signal(barrier, inc=1, device_id=at_z(d), device_id_type=MESH)
        pl.semaphore_signal(barrier, inc=1, device_id=at_plane(d), device_id_type=MESH)

    lane1 = lax.broadcasted_iota(jnp.int32, (1, 128), 1)
    ms[...] = jnp.zeros_like(ms)
    for load in loads[7:]:
        load.wait()
    for p in range(2):
        for g in range(8):
            xs[p * 8 + g : p * 8 + g + 1, :] = x_ref[p : p + 1, g * 1536 : (g + 1) * 1536].astype(F32)
        group = lax.broadcasted_iota(jnp.int32, (16, CYCLES), 0) == group_ref[p]
        inv = jnp.sum(jnp.where(group, noise_ref[...], 0.0), axis=0, keepdims=True)
        info = jnp.concatenate([inv, jnp.ones((1, 96), F32)], axis=1)
        for at, value in ((40, cen_ref[p, 0]), (41, cen_ref[p, 1]), (42, rot_ref[p])):
            info = jnp.where(lane1 == at, value.astype(F32), info)
        ms[p * 4 : p * 4 + 1, :] = info
    xb[...] = xs[...].astype(BF16)
    xg[c] = xb[...]
    mg[c] = ms[...]

    def remote(src, dst, ss, rs, dev):
        return pltpu.make_async_remote_copy(
            src_ref=src, dst_ref=dst, send_sem=ss, recv_sem=rs, device_id=dev, device_id_type=MESH
        )

    pw[...] = jnp.zeros_like(pw)
    loads[0].wait()

    def one_group(g, carry):
        at = pl.multiple_of(g * 1536, 1536)
        nat = [refs_ref[:, pl.ds(at + n * 128, 128)].astype(F32) for n in range(12)]
        blocks = to_blocks(nat)
        power = blocks[0] * blocks[0]
        for b in range(1, 12):
            power = power + blocks[b] * blocks[b]
        to = pl.multiple_of(g * 128, 128)
        pw[0:25, pl.ds(pl.multiple_of((g % 4) * 128, 128), 128)] += power
        for b in range(12):
            v = blocks[b].astype(BF16)
            j = (12 - b) % 12
            r2[j * 32 : j * 32 + 25, pl.ds(to, 128)] = v
            r2[(j + 12) * 32 : (j + 12) * 32 + 25, pl.ds(to, 128)] = v
        return carry

    lax.fori_loop(0, 8, one_group, 0)
    for b in range(12):
        a_ref[b * 256 + 192 : b * 256 + 256, :] = jnp.zeros((64, 1024), BF16)
    nb[...] = jnp.zeros_like(nb)
    ph2[...] = jnp.zeros_like(ph2)
    pl.semaphore_wait(barrier, 17)

    x_copies = []
    for d in range(1, 4):
        x_copies.append(remote(ms, mg.at[c], m_s.at[d], m_r.at[d], at_cls(d)))
        x_copies.append(remote(xb, xg.at[c], x_s.at[d], x_r.at[d], at_cls(d)))
    for copy in x_copies:
        copy.start()


    for load in loads[1:7]:
        load.wait()
    for copy in x_copies:
        copy.wait()

    for i in range(4):
        for n in range(12):
            at = n * 64 + i * 16
            xf[at : at + 16, :] = xg[i, :, n * 128 : n * 128 + 128].astype(F32)
    for i in range(4):
        fin[i * 8 : i * 8 + 8, :] = mg[i]
    info = fin[pl.ds(0, 8, stride=4), :]
    lane8 = lax.broadcasted_iota(jnp.int32, (8, 128), 1)
    cx, cy = info[:, 40:41], info[:, 41:42]
    turn = jnp.where(lane8 % 8 == lax.broadcasted_iota(jnp.int32, (8, 128), 0), info[:, 42:43], 0.0)
    turn = jnp.sum(turn, axis=0, keepdims=True)
    grow = (
        lax.broadcasted_iota(jnp.int32, (CYCLES, 512), 0)
        == lax.broadcasted_iota(jnp.int32, (CYCLES, 512), 1) // 16
    ).astype(F32)
    w512 = jnp.dot(info[:, 0:CYCLES], grow, preferred_element_type=F32, precision=HIGHEST)
    w = [w512[:, i * 128 : i * 128 + 128] for i in range(4)]

    def phase(value, row, b, gq):
        size = jnp.abs(value)
        cos, sin = jnp.ones((8, 128), F32), jnp.zeros((8, 128), F32)
        for m in (1, 2, 3):
            hit = size == float(m)
            at = row + (m - 1) * 2
            cos = jnp.where(hit, center_ref[b, at : at + 1, gq * 128 : gq * 128 + 128], cos)
            sin = jnp.where(hit, center_ref[b, at + 1 : at + 2, gq * 128 : gq * 128 + 128], sin)
        return cos, jnp.where(value < 0.0, -sin, sin)

    for gq in range(4):
        re = to_blocks([xf[pl.ds(n * 64 + gq, 8, stride=8), :] for n in range(12)])
        im = to_blocks([xf[pl.ds(n * 64 + gq + 4, 8, stride=8), :] for n in range(12)])
        for b in range(12):
            xc, xs = phase(cx, 0, b, gq)
            yc, ys = phase(cy, 6, b, gq)
            pc, ps = xc * yc - xs * ys, xc * ys + xs * yc
            u, v = re[b] * w[gq], im[b] * w[gq]
            yre[b, :, gq * 128 : gq * 128 + 128] = u * pc - v * ps
            yim[b, :, gq * 128 : gq * 128 + 128] = u * ps + v * pc

    def align(b):
        for l in range(4):
            cols = slice(l * 128, l * 128 + 128)
            u, v = yre[b, :, cols], yim[b, :, cols]
            for t in range(0, 25, 2):
                res, ims = [], []
                for tt in range(t, min(t + 2, 25)):
                    tc = shift_ref[b, tt : tt + 1, cols]
                    ts = shift_ref[b, 32 + tt : 33 + tt, cols]
                    res.append(u * tc - v * ts)
                    ims.append(u * ts + v * tc)
                if len(res) == 1:
                    res.append(jnp.zeros((8, 128), F32))
                    ims.append(jnp.zeros((8, 128), F32))
                at = slice(b * 256 + t * 8, b * 256 + t * 8 + 16)
                a_ref[at, cols] = jnp.concatenate(res, axis=0).astype(BF16)
                a_ref[at, l * 128 + 512 : l * 128 + 640] = jnp.concatenate(ims, axis=0).astype(BF16)

    def score(b):
        row = ((12 - b) % 12) * 32
        part = lax.dot_general(
            r2[row : row + 384, :], a_ref[b * 256 : b * 256 + 256, :],
            (((1,), (1,)), ((), ())), preferred_element_type=F32,
        )
        if b == 0:
            s_ref[...] = part
        else:
            s_ref[...] += part

    align(0)
    for b in range(12):
        if b < 11:
            align(b + 1)
        score(b)

    w128 = jnp.concatenate([w512] * 16, axis=0)
    pen = lax.dot_general(
        pw[...], w128, (((1,), (1,)), ((), ())), preferred_element_type=F32, precision=HIGHEST
    )
    mine = (
        lax.broadcasted_iota(jnp.int32, (KPAD, 100), 0) + c * 25
        == lax.broadcasted_iota(jnp.int32, (KPAD, 100), 1)
    )
    frac = jnp.sum(jnp.where(mine, frac_in[...], 0.0), axis=1, keepdims=True)
    base = jnp.log(jnp.where(frac > 0.0, frac, 1.0)) - 0.5 * pen
    base = jnp.concatenate([base, base], axis=1)
    away = lax.broadcasted_iota(jnp.int32, (16, 128), 0).astype(F32) - turn
    away = jnp.where(away < 0.0, away + 12.0, away)
    away = jnp.minimum(away, 12.0 - away)
    prior = -KAPPA * away * away
    prior = jnp.concatenate([prior, prior], axis=1)
    live = (lax.broadcasted_iota(jnp.int32, (KPAD, 256), 0) < 25) & (
        lax.broadcasted_iota(jnp.int32, (KPAD, 256), 1) < 200
    )
    top = jnp.full((KPAD, 256), -3e38, F32)
    for r in range(12):
        v = s_ref[r * 32 : r * 32 + 32, :] + (base + prior[r : r + 1, :])
        v = jnp.where(live, v, -3e38)
        s_ref[r * 32 : r * 32 + 32, :] = v
        top = jnp.maximum(top, v)
    here = fold(jnp.max(top, axis=0, keepdims=True), jnp.maximum)
    here256 = jnp.concatenate([here, here], axis=1)[0:1]
    total = jnp.zeros((KPAD, 256), F32)
    for r in range(12):
        v = jnp.where(live, jnp.exp(s_ref[r * 32 : r * 32 + 32, :] - here256), 0.0)
        s_ref[r * 32 : r * 32 + 32, :] = v
        total = total + v
    mass = fold(jnp.sum(total, axis=0, keepdims=True), jnp.add)
    sm_src[0:8] = here
    sm_src[8:16] = mass
    sm_copies = [remote(sm_src, sm.at[d], sm_s.at[d], sm_r.at[d], at_cls(d)) for d in range(1, 4)]
    for copy in sm_copies:
        copy.start()
    for copy in sm_copies:
        copy.wait()
    peak = here
    for d in range(1, 4):
        peak = jnp.maximum(peak, sm[d, 0:8])
    full = mass * jnp.exp(here - peak)
    for d in range(1, 4):
        full = full + sm[d, 8:16] * jnp.exp(sm[d, 0:8] - peak)
    evid = (peak + jnp.log(full))[0:1]
    first = jnp.sum(jnp.where(lane1 == 2 * c, evid, 0.0), axis=1, keepdims=True)
    second = jnp.sum(jnp.where(lane1 == 2 * c + 1, evid, 0.0), axis=1, keepdims=True)
    evid_ref[...] = jnp.where(lane1 == 0, first, second)[:, 0:2]
    scale = jnp.exp(here - peak) / full
    scale256 = jnp.concatenate([scale, scale], axis=1)[0:1]
    weight = jnp.zeros((KPAD, 256), F32)
    for r in range(12):
        v = s_ref[r * 32 : r * 32 + 32, :] * scale256
        weight = weight + v
        v = v.astype(BF16)
        for b1 in range(12):
            b = (b1 - r) % 12
            p2[b * 32 : b * 32 + 32, b1 * 256 : b1 * 256 + 256] = v

    inv256 = jnp.concatenate([info] * 32, axis=0)
    dsrc[...] = lax.dot_general(
        weight, inv256, (((1,), (0,)), ((), ())), preferred_element_type=F32, precision=HIGHEST
    )
    dz_copies = [remote(dsrc, dz.at[d], dz_s.at[d], dz_r.at[d], at_z(d)) for d in range(1, 8)]
    for copy in dz_copies:
        copy.start()

    def weighted(d, width):
        offs = [pl.multiple_of(((h + d + e) % 8) * 128, 128) for e in range(width)]
        rhs = jnp.concatenate([a_ref[:, pl.ds(o, 128)] for o in offs], axis=1)
        n_ref[...] = jnp.dot(p2[...], rhs, preferred_element_type=F32)
        for e in range(2):
            for b in range(12):
                nb[pl.ds(e * ROWS + b, 25, stride=12), :] = n_ref[
                    b * 32 : b * 32 + 25, e * 128 : e * 128 + 128
                ]

    def rs1_copy(d):
        return remote(sb.at[d], rs1.at[d], rs1_s.at[d], rs1_r.at[d], at_plane(d))

    def send_sum(d, e):
        encode(nb[e * ROWS : e * ROWS + ROWS, :], sb.at[d])
        rs1_copy(d).start()

    def one_pair(i, carry):
        weighted(2 * i + 1, 2)
        send_sum(2 * i + 1, 0)
        send_sum(2 * i + 2, 1)
        return carry

    lax.fori_loop(0, 3, one_pair, 0)
    weighted(7, 2)
    send_sum(7, 0)
    acc[...] = nb[ROWS : 2 * ROWS, :]
    rs1_copies = [rs1_copy(d) for d in range(1, 8)]

    for copy in dz_copies:
        copy.wait()
    dsum = dsrc[...]
    for d in range(1, 8):
        dsum = dsum + dz[d]
    dpsrc[...] = dsum
    dp_copies = [remote(dpsrc, dp.at[d], dp_s.at[d], dp_r.at[d], at_plane(d)) for d in range(1, 8)]
    for copy in dp_copies:
        copy.start()

    tot = acc[...]
    for d in range(1, 8):
        rs1_copies[d - 1].wait_recv()
        tot = tot + decode(rs1.at[d])
    tot = jnp.where(lax.broadcasted_iota(jnp.int32, (ROWS, 128), 0) < 300, tot, 0.0)
    ph2[0:ROWS, :] = tot
    code, power = encode_rows(tot)
    ph2c[0:ROWS, :] = code
    ph2e[...] = power

    def sized(zs, make, act):
        @pl.when(zs < 6)
        def _():
            act(make(SLOT))

        @pl.when(zs == 6)
        def _():
            act(make(16))

    def rs2_copy(d):
        def make(size):
            at = pl.multiple_of(((z + d) % 8) * SLOT, 16)
            return remote(
                ph2c.at[pl.ds(at, size)], rs2.at[d, pl.ds(0, size)], rs2_s.at[d], rs2_r.at[d], at_z(d)
            )

        return make

    re_copies = [remote(ph2e, rs2e.at[d], re_s.at[d], re_r.at[d], at_z(d)) for d in range(1, 8)]
    for d in range(1, 8):
        sized((z + d) % 8, rs2_copy(d), lambda copy: copy.start())
        re_copies[d - 1].start()
    for copy in dp_copies:
        copy.wait()
    dsum = dpsrc[...]
    for d in range(1, 8):
        dsum = dsum + dp[d]
    square = (
        lax.broadcasted_iota(jnp.int32, (KPAD, KPAD), 0)
        == lax.broadcasted_iota(jnp.int32, (KPAD, KPAD), 1)
    )
    frac = jnp.sum(jnp.where(square, dsum[:, 32:33], 0.0), axis=0, keepdims=True)
    frac_ref[...] = frac[:, 0:25] * (1.0 / 512.0)
    rho = lax.broadcasted_iota(jnp.int32, (CYCLES, 128), 0)
    lane = lax.broadcasted_iota(jnp.int32, (CYCLES, 128), 1)
    pick = (rho == (h % 4) * 8 + lane // 16).astype(F32)
    mine = lax.broadcasted_iota(jnp.int32, (SLOT, KPAD), 0) // 12 + z * 4
    mine = (mine == lax.broadcasted_iota(jnp.int32, (SLOT, KPAD), 1)).astype(F32)
    div = jnp.dot(dsum[:, 0:CYCLES] + reg_ref[...], pick, preferred_element_type=F32, precision=HIGHEST)
    div = jnp.dot(mine, div, preferred_element_type=F32, precision=HIGHEST)
    own = pl.multiple_of(z * SLOT, 16)
    tot = ph2[pl.ds(own, SLOT), :]
    for d in range(1, 8):
        sized(z, rs2_copy(d), lambda copy: copy.wait_recv())
        re_copies[d - 1].wait_recv()
        tot = tot + rs2[d].astype(jnp.int32).astype(F32) * jnp.exp2(rs2e[d])
    inside = lax.broadcasted_iota(jnp.int32, (SLOT, 128), 0) // 12 + z * 4 < 25
    tot = jnp.where(inside, tot / jnp.where(inside, div, 1.0), 0.0)

    high = tot.astype(BF16)
    low = (tot - high.astype(F32)).astype(BF16)
    wide = jnp.dot(jnp.concatenate([high, low], axis=0), spread_ref[...], preferred_element_type=F32)
    brow = lax.broadcasted_iota(jnp.int32, (SLOT, 128), 0) % 12
    slot = lax.broadcasted_iota(jnp.int32, (SLOT, 128), 1) // 16
    stack = jnp.concatenate(
        [
            jnp.concatenate(
                [
                    jnp.where(
                        slot == (4 * r + brow) % 8,
                        wide[i * SLOT : (i + 1) * SLOT, r * 128 : r * 128 + 128],
                        0.0,
                    )
                    for i in range(2)
                ],
                axis=1,
            )
            for r in range(8)
        ],
        axis=0,
    ).astype(BF16)
    both = jnp.dot(rows_ref[...], stack, preferred_element_type=F32)
    code, power = encode_rows(both[:, 0:128] + both[:, 128:256])
    agc[z] = code
    age[z] = power

    def ag1_copy(d):
        def make(size):
            mine = agc.at[z, pl.ds(0, size)]
            return remote(mine, mine, ag1_s.at[d], ag1_r.at[d], at_z(d))

        return make

    def ag2_copy(dz_, d):
        def make(size):
            zs = (z + 8 - dz_) % 8
            return remote(
                agc.at[zs, pl.ds(0, size)],
                gc.at[h, zs, pl.ds(0, size)],
                ag2_s.at[dz_, d],
                ag2_r.at[dz_, d],
                at_plane(d),
            )

        return make

    ae_copies = [remote(age.at[z], age.at[z], ae_s.at[d], ae_r.at[d], at_z(d)) for d in range(1, 8)]
    ge_copies = [remote(age, ge.at[h], ge_s.at[d], ge_r.at[d], at_plane(d)) for d in range(1, 8)]
    for d in range(1, 8):
        sized(z, ag1_copy(d), lambda copy: copy.start())
        ae_copies[d - 1].start()
    for d in range(1, 8):
        sized(z, ag2_copy(0, d), lambda copy: copy.start())
    for dz_ in range(1, 8):
        zs = (z + 8 - dz_) % 8
        sized(zs, ag1_copy(dz_), lambda copy: copy.wait_recv())
        for d in range(1, 8):
            sized(zs, ag2_copy(dz_, d), lambda copy: copy.start())
        ae_copies[dz_ - 1].wait_recv()
    for copy in ge_copies:
        copy.start()

    own_copies = [
        pltpu.make_async_copy(agc, gc.at[h], in_s.at[12]),
        pltpu.make_async_copy(age, ge.at[h], in_s.at[13]),
    ]
    for copy in own_copies:
        copy.start()
    for d in range(1, 8):
        for dz_ in range(8):
            sized((z + 8 - dz_) % 8, ag2_copy(dz_, d), lambda copy: copy.wait_recv())
        ge_copies[d - 1].wait_recv()
    for copy in own_copies:
        copy.wait()
    for d in range(1, 8):
        sized((z + d) % 8, rs2_copy(d), lambda copy: copy.wait_send())
        sized(z, ag1_copy(d), lambda copy: copy.wait_send())
        for dz_ in range(8):
            sized((z + 8 - dz_) % 8, ag2_copy(dz_, d), lambda copy: copy.wait_send())
    for copy in rs1_copies + re_copies + ae_copies + ge_copies:
        copy.wait_send()


def finish(code_ref, power_ref, frac_in, evid_in, out_ref, frac_ref, evid_ref, fin):
    for g in range(4):
        for zs in range(7):
            code = code_ref[g, zs].astype(jnp.int32).astype(F32)
            fin[zs * SLOT : (zs + 1) * SLOT, :] = code * jnp.exp2(power_ref[g, zs])
        for n in range(12):
            at = g * 1536 + n * 128
            out_ref[:, at : at + 128] = fin[pl.ds(n, 25, stride=12), :]
    frac_ref[...] = frac_in[...]
    evid_ref[...] = evid_in[...]


def step(particles, references, centers, rot_prior, groups, class_frac, inv_noise, reg_inv):
    shift, center = tables()
    spread, rows = shard_maps()
    vmem = pl.BlockSpec(memory_space=pltpu.VMEM)
    dma = pltpu.SemaphoreType.DMA
    hbm = pl.BlockSpec(memory_space=pltpu.HBM)
    code, power, frac, evid = pl.pallas_call(
        kernel,
        out_shape=(
            jax.ShapeDtypeStruct((8, 8, SLOT, 128), jnp.int16),
            jax.ShapeDtypeStruct((8, 8, 1, 128), F32),
            jax.ShapeDtypeStruct((1, 25), F32),
            jax.ShapeDtypeStruct((1, 2), F32),
        ),
        in_specs=[hbm] * 12,
        out_specs=(hbm, hbm, vmem, vmem),
        scratch_shapes=[
            pltpu.VMEM((2, FEAT), BF16),
            pltpu.SMEM((2, 2), jnp.int32),
            pltpu.SMEM((2,), jnp.int32),
            pltpu.SMEM((2,), jnp.int32),
            pltpu.VMEM((1, 100), F32),
            pltpu.VMEM((16, CYCLES), F32),
            pltpu.VMEM((1, CYCLES), F32),
            pltpu.VMEM((25, FEAT), BF16),
            pltpu.VMEM((12, 64, 512), F32),
            pltpu.VMEM((12, 16, 512), F32),
            pltpu.VMEM((128, 1024), BF16),
            pltpu.VMEM((SLOT, 8 * SLOT), BF16),
            pltpu.VMEM((16, 1536), F32),
            pltpu.VMEM((8, 128), F32),
            pltpu.VMEM((16, 1536), BF16),
            pltpu.VMEM((4, 16, 1536), BF16),
            pltpu.VMEM((4, 8, 128), F32),
            pltpu.VMEM((12 * 64, 128), F32),
            pltpu.VMEM((12, 8, 512), F32),
            pltpu.VMEM((12, 8, 512), F32),
            pltpu.VMEM((12 * 256, 1024), BF16),
            pltpu.VMEM((24 * 32, 1024), BF16),
            pltpu.VMEM((KPAD, 512), F32),
            pltpu.VMEM((384, 256), F32),
            pltpu.VMEM((16, 128), F32),
            pltpu.VMEM((4, 16, 128), F32),
            pltpu.VMEM((384, 12 * 256), BF16),
            pltpu.VMEM((384, 256), F32),
            pltpu.VMEM((2 * ROWS, 128), F32),
            pltpu.VMEM((8, ROWS, 128), jnp.int16),
            pltpu.VMEM((8, ROWS, 128), jnp.int16),
            pltpu.VMEM((ROWS, 128), F32),
            pltpu.VMEM((8 * SLOT, 128), F32),
            pltpu.VMEM((8 * SLOT, 128), jnp.int16),
            pltpu.VMEM((1, 128), F32),
            pltpu.VMEM((8, SLOT, 128), jnp.int16),
            pltpu.VMEM((8, 1, 128), F32),
            pltpu.VMEM((8, SLOT, 128), jnp.int16),
            pltpu.VMEM((8, 1, 128), F32),
            pltpu.VMEM((KPAD, 128), F32),
            pltpu.VMEM((KPAD, 128), F32),
            pltpu.VMEM((8, KPAD, 128), F32),
            pltpu.VMEM((KPAD, 128), F32),
            pltpu.VMEM((8, KPAD, 128), F32),
            dma((14,)),
        ]
        + [dma((4,))] * 6
        + [dma((8,))] * 6
        + [dma((8, 8))] * 2
        + [dma((8,))] * 10,
        compiler_params=pltpu.CompilerParams(
            collective_id=0, has_side_effects=True, vmem_limit_bytes=60 * 1024 * 1024
        ),
    )(
        particles, centers, rot_prior, groups, class_frac.reshape(1, 100), inv_noise,
        reg_inv.reshape(1, CYCLES), references, jnp.asarray(shift), jnp.asarray(center),
        jnp.asarray(spread, BF16), jnp.asarray(rows, BF16),
    )
    one = lambda shape: pl.BlockSpec(shape, lambda g: (0,) * len(shape))
    out, frac, evid = pl.pallas_call(
        finish,
        grid=(2,),
        out_shape=(
            jax.ShapeDtypeStruct((25, FEAT), F32),
            jax.ShapeDtypeStruct((1, 25), F32),
            jax.ShapeDtypeStruct((1, 2), F32),
        ),
        in_specs=[
            pl.BlockSpec((4, 8, SLOT, 128), lambda g: (g, 0, 0, 0)),
            pl.BlockSpec((4, 8, 1, 128), lambda g: (g, 0, 0, 0)),
            one((1, 25)),
            one((1, 2)),
        ],
        out_specs=(pl.BlockSpec((25, 6144), lambda g: (0, g)), one((1, 25)), one((1, 2))),
        scratch_shapes=[pltpu.VMEM((8 * SLOT, 128), F32)],
        compiler_params=pltpu.CompilerParams(vmem_limit_bytes=60 * 1024 * 1024),
    )(code, power, frac, evid)
    return out, frac.reshape(25), evid.reshape(2)


def solution(mesh):
    both = ("cls", "ptl")
    return jax.shard_map(
        step,
        mesh=mesh,
        in_specs=(P(both, None), P("cls", None), P(both, None), P(both), P(both), P(), P(), P()),
        out_specs=(P("cls", None), P("cls"), P(both)),
        check_vma=False,
    )
```

```python
import math

import jax
import jax.numpy as jnp
import numpy as np
from jax import lax
from jax.experimental import pallas as pl
from jax.experimental.pallas import tpu as pltpu
from jax.sharding import PartitionSpec as P

ROTS = 12
SPAN = 2
CYCLES = 32
ANGLES = 192
BOX = 128
SHIFTS = 25
FEAT = 12288
KAPPA = 0.25
HIGHEST = lax.Precision.HIGHEST
MESH = pl.DeviceIdType.MESH
F32, BF16 = jnp.float32, jnp.bfloat16

KPAD = 32
ROWS = 304
HEAD = 32
SLOT = 48


def tables():
    cycle = np.arange(CYCLES, dtype=np.float64) + 1.0
    angle = np.arange(ANGLES, dtype=np.float64) * (2.0 * math.pi / ANGLES)
    fx = cycle[:, None] * np.cos(angle)[None] / BOX
    fy = cycle[:, None] * np.sin(angle)[None] / BOX

    def blocked(v):
        n = v.shape[0]
        v = v.reshape(n, 4, 8, 12, 16)
        return np.transpose(v, (3, 0, 1, 2, 4)).reshape(12, n, 512)

    t = np.arange(SHIFTS)
    mx, my = t // 5 - SPAN, t % 5 - SPAN
    ph = 2.0 * math.pi * (mx[:, None, None] * fx + my[:, None, None] * fy)
    shift = np.concatenate([np.cos(ph), np.zeros((7, 32, 192)), np.sin(ph), np.zeros((7, 32, 192))])
    rows = []
    for f in (fx, fy):
        for m in (1, 2, 3):
            rows += [np.cos(2.0 * math.pi * m * f), np.sin(2.0 * math.pi * m * f)]
    center = np.stack(rows + [np.zeros_like(fx)] * 4)
    return blocked(shift).astype(np.float32), blocked(center).astype(np.float32)


def shard_maps():
    spread = np.zeros((128, 1024), np.float32)
    for rho in range(8):
        for j in range(8):
            for s in range(16):
                spread[rho * 16 + s, rho * 128 + j * 16 + s] = 1
    rows = np.zeros((SLOT, 8 * SLOT), np.float32)
    for rho in range(8):
        for k in range(4):
            for b in range(12):
                rows[k * 12 + (12 * rho + b) // 8, rho * SLOT + k * 12 + b] = 1
    return spread, rows


def to_blocks(nat):
    lane = lax.broadcasted_iota(jnp.int32, nat[0].shape, 1) // 16
    out = []
    for b in range(12):
        acc = None
        for rho in range(8):
            n, j = divmod(12 * rho + b, 8)
            v = nat[n] if j == rho else pltpu.roll(nat[n], (16 * (rho - j)) % 128, 1)
            acc = v if acc is None else jnp.where(lane == rho, v, acc)
        out.append(acc)
    return out


def fold(v, op):
    v = jnp.broadcast_to(op(v[:, :128], v[:, 128:]), (8, 128))
    for step in (8, 16, 32, 64):
        v = op(v, pltpu.roll(v, step, 1))
    return v


def encode(value, to):
    top = jnp.max(jnp.abs(value), axis=0, keepdims=True)
    power = jnp.ceil(jnp.log2(jnp.maximum(top, 1e-30)) + 1e-3) - 15.0
    code = jnp.round(value * jnp.exp2(-power))
    row = lax.broadcasted_iota(jnp.int32, value.shape, 0)
    to[...] = jnp.where(row == 300, power, code).astype(jnp.int32).astype(jnp.int16)


def decode(code):
    value = code[...].astype(jnp.int32).astype(F32)
    return value * jnp.exp2(value[300:301])


def encode_rows(value):
    top = jnp.max(jnp.abs(value), axis=0, keepdims=True)
    power = jnp.ceil(jnp.log2(jnp.maximum(top, 1e-30)) + 1e-3) - 15.0
    code = jnp.round(value * jnp.exp2(-power)).astype(jnp.int32).astype(jnp.int16)
    return code, power


def kernel(
    x_hbm, cen_hbm, rot_hbm, group_hbm, frac_hbm, noise_hbm, reg_hbm,
    refs_hbm, shift_hbm, center_hbm, spread_hbm, rows_hbm,
    gp, gz, ge, frac_ref, evid_ref,
    x_ref, cen_ref, rot_ref, group_ref, frac_in, noise_ref, reg_ref,
    refs_ref, shift_ref, center_ref, spread_ref, rows_ref,
    xs, ms, xb, xg, mg, xf, yre, yim, a_ref, r2, pw, s_ref, sm_src, sm, p2, n_ref, nb, sb, rs1, acc,
    ph2, ph2c, ph2e, rs2, rs2e, agp, agz, age, fin, dsrc, dz, dpsrc, dp, in_s,
    x_s, x_r, m_s, m_r, sm_s, sm_r, rs1_s, rs1_r, rs2_s, rs2_r, ag1_s, ag1_r, ag2_s, ag2_r, re_s, re_r, ae_s, ae_r, ge_s, ge_r,
    az_s, az_r, gz_s, gz_r,
    dz_s, dz_r, dp_s, dp_r,
):
    c = lax.axis_index("cls")
    q = lax.axis_index("ptl")
    h, z = q // 8, q % 8

    def at_cls(d):
        return ((c + d) % 4, q)

    def at_z(d):
        return (c, h * 8 + (z + d) % 8)

    def at_plane(d):
        return (c, ((h + d) % 8) * 8 + z)

    loads = [
        pltpu.make_async_copy(src, dst, in_s.at[i])
        for i, (src, dst) in enumerate(
            (
                (refs_hbm, refs_ref), (center_hbm, center_ref), (shift_hbm, shift_ref),
                (spread_hbm, spread_ref), (rows_hbm, rows_ref),
                (frac_hbm, frac_in), (reg_hbm, reg_ref),
                (cen_hbm, cen_ref), (rot_hbm, rot_ref), (group_hbm, group_ref),
                (noise_hbm, noise_ref), (x_hbm, x_ref),
            )
        )
    ]
    for load in loads[::-1]:
        load.start()
    barrier = pltpu.get_barrier_semaphore()
    for d in range(1, 4):
        pl.semaphore_signal(barrier, inc=1, device_id=at_cls(d), device_id_type=MESH)
    for d in range(1, 8):
        pl.semaphore_signal(barrier, inc=1, device_id=at_z(d), device_id_type=MESH)
        pl.semaphore_signal(barrier, inc=1, device_id=at_plane(d), device_id_type=MESH)

    lane1 = lax.broadcasted_iota(jnp.int32, (1, 128), 1)
    ms[...] = jnp.zeros_like(ms)
    for load in loads[7:]:
        load.wait()
    for p in range(2):
        for g in range(8):
            xs[p * 8 + g : p * 8 + g + 1, :] = x_ref[p : p + 1, g * 1536 : (g + 1) * 1536].astype(F32)
        group = lax.broadcasted_iota(jnp.int32, (16, CYCLES), 0) == group_ref[p]
        inv = jnp.sum(jnp.where(group, noise_ref[...], 0.0), axis=0, keepdims=True)
        info = jnp.concatenate([inv, jnp.ones((1, 96), F32)], axis=1)
        for at, value in ((40, cen_ref[p, 0]), (41, cen_ref[p, 1]), (42, rot_ref[p])):
            info = jnp.where(lane1 == at, value.astype(F32), info)
        ms[p * 4 : p * 4 + 1, :] = info
    xb[...] = xs[...].astype(BF16)
    xg[c] = xb[...]
    mg[c] = ms[...]

    def remote(src, dst, ss, rs, dev):
        return pltpu.make_async_remote_copy(
            src_ref=src, dst_ref=dst, send_sem=ss, recv_sem=rs, device_id=dev, device_id_type=MESH
        )

    pl.semaphore_wait(barrier, 17)

    x_copies = []
    for d in range(1, 4):
        x_copies.append(remote(ms, mg.at[c], m_s.at[d], m_r.at[d], at_cls(d)))
        x_copies.append(remote(xb, xg.at[c], x_s.at[d], x_r.at[d], at_cls(d)))
    for copy in x_copies:
        copy.start()

    pw[...] = jnp.zeros_like(pw)
    loads[0].wait()

    def one_group(g, carry):
        at = pl.multiple_of(g * 1536, 1536)
        nat = [refs_ref[:, pl.ds(at + n * 128, 128)].astype(F32) for n in range(12)]
        blocks = to_blocks(nat)
        power = blocks[0] * blocks[0]
        for b in range(1, 12):
            power = power + blocks[b] * blocks[b]
        to = pl.multiple_of(g * 128, 128)
        pw[0:25, pl.ds(pl.multiple_of((g % 4) * 128, 128), 128)] += power
        for b in range(12):
            v = blocks[b].astype(BF16)
            j = (12 - b) % 12
            r2[j * 32 : j * 32 + 25, pl.ds(to, 128)] = v
            r2[(j + 12) * 32 : (j + 12) * 32 + 25, pl.ds(to, 128)] = v
        return carry

    lax.fori_loop(0, 8, one_group, 0)
    for b in range(12):
        a_ref[b * 256 + 192 : b * 256 + 256, :] = jnp.zeros((64, 1024), BF16)
    nb[...] = jnp.zeros_like(nb)
    ph2[...] = jnp.zeros_like(ph2)
    ph2c[...] = jnp.zeros_like(ph2c)
    for load in loads[1:7]:
        load.wait()
    for copy in x_copies:
        copy.wait()

    for i in range(4):
        for n in range(12):
            at = n * 64 + i * 16
            xf[at : at + 16, :] = xg[i, :, n * 128 : n * 128 + 128].astype(F32)
    for i in range(4):
        fin[i * 8 : i * 8 + 8, :] = mg[i]
    info = fin[pl.ds(0, 8, stride=4), :]
    lane8 = lax.broadcasted_iota(jnp.int32, (8, 128), 1)
    cx, cy = info[:, 40:41], info[:, 41:42]
    turn = jnp.where(lane8 % 8 == lax.broadcasted_iota(jnp.int32, (8, 128), 0), info[:, 42:43], 0.0)
    turn = jnp.sum(turn, axis=0, keepdims=True)
    grow = (
        lax.broadcasted_iota(jnp.int32, (CYCLES, 512), 0)
        == lax.broadcasted_iota(jnp.int32, (CYCLES, 512), 1) // 16
    ).astype(F32)
    w512 = jnp.dot(info[:, 0:CYCLES], grow, preferred_element_type=F32, precision=HIGHEST)
    w = [w512[:, i * 128 : i * 128 + 128] for i in range(4)]

    def phase(value, row, b, gq):
        size = jnp.abs(value)
        cos, sin = jnp.ones((8, 128), F32), jnp.zeros((8, 128), F32)
        for m in (1, 2, 3):
            hit = size == float(m)
            at = row + (m - 1) * 2
            cos = jnp.where(hit, center_ref[b, at : at + 1, gq * 128 : gq * 128 + 128], cos)
            sin = jnp.where(hit, center_ref[b, at + 1 : at + 2, gq * 128 : gq * 128 + 128], sin)
        return cos, jnp.where(value < 0.0, -sin, sin)

    for gq in range(4):
        re = to_blocks([xf[pl.ds(n * 64 + gq, 8, stride=8), :] for n in range(12)])
        im = to_blocks([xf[pl.ds(n * 64 + gq + 4, 8, stride=8), :] for n in range(12)])
        for b in range(12):
            xc, xs = phase(cx, 0, b, gq)
            yc, ys = phase(cy, 6, b, gq)
            pc, ps = xc * yc - xs * ys, xc * ys + xs * yc
            u, v = re[b] * w[gq], im[b] * w[gq]
            yre[b, :, gq * 128 : gq * 128 + 128] = u * pc - v * ps
            yim[b, :, gq * 128 : gq * 128 + 128] = u * ps + v * pc

    def align(b):
        for l in range(4):
            cols = slice(l * 128, l * 128 + 128)
            u, v = yre[b, :, cols], yim[b, :, cols]
            for t in range(0, 25, 2):
                res, ims = [], []
                for tt in range(t, min(t + 2, 25)):
                    tc = shift_ref[b, tt : tt + 1, cols]
                    ts = shift_ref[b, 32 + tt : 33 + tt, cols]
                    res.append(u * tc - v * ts)
                    ims.append(u * ts + v * tc)
                if len(res) == 1:
                    res.append(jnp.zeros((8, 128), F32))
                    ims.append(jnp.zeros((8, 128), F32))
                at = slice(b * 256 + t * 8, b * 256 + t * 8 + 16)
                a_ref[at, cols] = jnp.concatenate(res, axis=0).astype(BF16)
                a_ref[at, l * 128 + 512 : l * 128 + 640] = jnp.concatenate(ims, axis=0).astype(BF16)

    def score(b):
        row = ((12 - b) % 12) * 32
        part = lax.dot_general(
            r2[row : row + 384, :], a_ref[b * 256 : b * 256 + 256, :],
            (((1,), (1,)), ((), ())), preferred_element_type=F32,
        )
        if b == 0:
            s_ref[...] = part
        else:
            s_ref[...] += part

    align(0)
    for b in range(12):
        if b < 11:
            align(b + 1)
        score(b)

    w128 = jnp.concatenate([w512] * 16, axis=0)
    pen = lax.dot_general(
        pw[...], w128, (((1,), (1,)), ((), ())), preferred_element_type=F32, precision=HIGHEST
    )
    mine = (
        lax.broadcasted_iota(jnp.int32, (KPAD, 100), 0) + c * 25
        == lax.broadcasted_iota(jnp.int32, (KPAD, 100), 1)
    )
    frac = jnp.sum(jnp.where(mine, frac_in[...], 0.0), axis=1, keepdims=True)
    base = jnp.log(jnp.where(frac > 0.0, frac, 1.0)) - 0.5 * pen
    base = jnp.concatenate([base, base], axis=1)
    away = lax.broadcasted_iota(jnp.int32, (16, 128), 0).astype(F32) - turn
    away = jnp.where(away < 0.0, away + 12.0, away)
    away = jnp.minimum(away, 12.0 - away)
    prior = -KAPPA * away * away
    prior = jnp.concatenate([prior, prior], axis=1)
    live = (lax.broadcasted_iota(jnp.int32, (KPAD, 256), 0) < 25) & (
        lax.broadcasted_iota(jnp.int32, (KPAD, 256), 1) < 200
    )
    top = jnp.full((KPAD, 256), -3e38, F32)
    for r in range(12):
        v = s_ref[r * 32 : r * 32 + 32, :] + (base + prior[r : r + 1, :])
        v = jnp.where(live, v, -3e38)
        s_ref[r * 32 : r * 32 + 32, :] = v
        top = jnp.maximum(top, v)
    here = fold(jnp.max(top, axis=0, keepdims=True), jnp.maximum)
    here256 = jnp.concatenate([here, here], axis=1)[0:1]
    total = jnp.zeros((KPAD, 256), F32)
    for r in range(12):
        v = jnp.where(live, jnp.exp(s_ref[r * 32 : r * 32 + 32, :] - here256), 0.0)
        s_ref[r * 32 : r * 32 + 32, :] = v
        total = total + v
    mass = fold(jnp.sum(total, axis=0, keepdims=True), jnp.add)
    sm_src[0:8] = here
    sm_src[8:16] = mass
    sm_copies = [remote(sm_src, sm.at[d], sm_s.at[d], sm_r.at[d], at_cls(d)) for d in range(1, 4)]
    for copy in sm_copies:
        copy.start()
    for copy in sm_copies:
        copy.wait()
    peak = here
    for d in range(1, 4):
        peak = jnp.maximum(peak, sm[d, 0:8])
    full = mass * jnp.exp(here - peak)
    for d in range(1, 4):
        full = full + sm[d, 8:16] * jnp.exp(sm[d, 0:8] - peak)
    evid = (peak + jnp.log(full))[0:1]
    first = jnp.sum(jnp.where(lane1 == 2 * c, evid, 0.0), axis=1, keepdims=True)
    second = jnp.sum(jnp.where(lane1 == 2 * c + 1, evid, 0.0), axis=1, keepdims=True)
    evid_ref[...] = jnp.where(lane1 == 0, first, second)[:, 0:2]
    scale = jnp.exp(here - peak) / full
    scale256 = jnp.concatenate([scale, scale], axis=1)[0:1]
    weight = jnp.zeros((KPAD, 256), F32)
    for r in range(12):
        v = s_ref[r * 32 : r * 32 + 32, :] * scale256
        weight = weight + v
        v = v.astype(BF16)
        for b1 in range(12):
            b = (b1 - r) % 12
            p2[b * 32 : b * 32 + 32, b1 * 256 : b1 * 256 + 256] = v

    inv256 = jnp.concatenate([info] * 32, axis=0)
    dsrc[...] = lax.dot_general(
        weight, inv256, (((1,), (0,)), ((), ())), preferred_element_type=F32, precision=HIGHEST
    )
    dz_copies = [remote(dsrc, dz.at[d], dz_s.at[d], dz_r.at[d], at_z(d)) for d in range(1, 8)]
    for copy in dz_copies:
        copy.start()

    def weighted(d, width):
        offs = [pl.multiple_of(((h + d + e) % 8) * 128, 128) for e in range(width)]
        rhs = jnp.concatenate([a_ref[:, pl.ds(o, 128)] for o in offs], axis=1)
        n_ref[...] = jnp.dot(p2[...], rhs, preferred_element_type=F32)
        for e in range(2):
            for b in range(12):
                nb[pl.ds(e * ROWS + b, 25, stride=12), :] = n_ref[
                    b * 32 : b * 32 + 25, e * 128 : e * 128 + 128
                ]

    def rs1_copy(d):
        return remote(sb.at[d], rs1.at[d], rs1_s.at[d], rs1_r.at[d], at_plane(d))

    def send_sum(d, e):
        encode(nb[e * ROWS : e * ROWS + ROWS, :], sb.at[d])
        rs1_copy(d).start()

    def one_pair(i, carry):
        weighted(2 * i + 1, 2)
        send_sum(2 * i + 1, 0)
        send_sum(2 * i + 2, 1)
        return carry

    lax.fori_loop(0, 3, one_pair, 0)
    weighted(7, 2)
    send_sum(7, 0)
    acc[...] = nb[ROWS : 2 * ROWS, :]
    rs1_copies = [rs1_copy(d) for d in range(1, 8)]

    for copy in dz_copies:
        copy.wait()
    dsum = dsrc[...]
    for d in range(1, 8):
        dsum = dsum + dz[d]
    dpsrc[...] = dsum
    dp_copies = [remote(dpsrc, dp.at[d], dp_s.at[d], dp_r.at[d], at_plane(d)) for d in range(1, 8)]
    for copy in dp_copies:
        copy.start()

    tot = acc[...]
    for d in range(1, 8):
        rs1_copies[d - 1].wait_recv()
        tot = tot + decode(rs1.at[d])
    tot = jnp.where(lax.broadcasted_iota(jnp.int32, (ROWS, 128), 0) < 300, tot, 0.0)
    ph2[0:ROWS, :] = tot
    code, power = encode_rows(tot)
    ph2c[0:ROWS, :] = code
    ph2e[...] = power

    far = (4, 3, 5, 2, 6, 1, 7)
    re_copies = {d: remote(ph2e, rs2e.at[d], re_s.at[d], re_r.at[d], at_z(d)) for d in far}
    rs2_copies = {}
    for d in far:
        at = pl.multiple_of(((z + d) % 8) * SLOT, 16)
        rs2_copies[d] = remote(
            ph2c.at[pl.ds(at, SLOT)], rs2.at[d], rs2_s.at[d], rs2_r.at[d], at_z(d)
        )
        rs2_copies[d].start()
        re_copies[d].start()
    for copy in dp_copies:
        copy.wait()
    dsum = dpsrc[...]
    for d in range(1, 8):
        dsum = dsum + dp[d]
    square = (
        lax.broadcasted_iota(jnp.int32, (KPAD, KPAD), 0)
        == lax.broadcasted_iota(jnp.int32, (KPAD, KPAD), 1)
    )
    frac = jnp.sum(jnp.where(square, dsum[:, 32:33], 0.0), axis=0, keepdims=True)
    frac_ref[...] = frac[:, 0:25] * (1.0 / 512.0)
    rho = lax.broadcasted_iota(jnp.int32, (CYCLES, 128), 0)
    lane = lax.broadcasted_iota(jnp.int32, (CYCLES, 128), 1)
    pick = (rho == (h % 4) * 8 + lane // 16).astype(F32)
    mine = lax.broadcasted_iota(jnp.int32, (SLOT, KPAD), 0) // 12 + z * 4
    mine = (mine == lax.broadcasted_iota(jnp.int32, (SLOT, KPAD), 1)).astype(F32)
    div = jnp.dot(dsum[:, 0:CYCLES] + reg_ref[...], pick, preferred_element_type=F32, precision=HIGHEST)
    div = jnp.dot(mine, div, preferred_element_type=F32, precision=HIGHEST)
    own = pl.multiple_of(z * SLOT, 16)
    tot = ph2[pl.ds(own, SLOT), :]
    for d in range(1, 8):
        rs2_copies[d].wait_recv()
        re_copies[d].wait_recv()
        tot = tot + rs2[d].astype(jnp.int32).astype(F32) * jnp.exp2(rs2e[d])
    inside = lax.broadcasted_iota(jnp.int32, (SLOT, 128), 0) // 12 + z * 4 < 25
    tot = jnp.where(inside, tot / jnp.where(inside, div, 1.0), 0.0)

    high = tot.astype(BF16)
    low = (tot - high.astype(F32)).astype(BF16)
    wide = jnp.dot(jnp.concatenate([high, low], axis=0), spread_ref[...], preferred_element_type=F32)
    brow = lax.broadcasted_iota(jnp.int32, (SLOT, 128), 0) % 12
    slot = lax.broadcasted_iota(jnp.int32, (SLOT, 128), 1) // 16
    stack = jnp.concatenate(
        [
            jnp.concatenate(
                [
                    jnp.where(
                        slot == (4 * r + brow) % 8,
                        wide[i * SLOT : (i + 1) * SLOT, r * 128 : r * 128 + 128],
                        0.0,
                    )
                    for i in range(2)
                ],
                axis=1,
            )
            for r in range(8)
        ],
        axis=0,
    ).astype(BF16)
    both = jnp.dot(rows_ref[...], stack, preferred_element_type=F32)
    code, power = encode_rows(both[:, 0:128] + both[:, 128:256])
    first = pl.multiple_of(z * HEAD, HEAD)
    agp[pl.ds(first, HEAD), :] = code[0:HEAD]
    agz[h] = code[HEAD:SLOT]
    age[z] = power

    head = agp.at[pl.ds(first, HEAD)]
    used = pl.ds(0, 6 * HEAD + 16)
    ag1_copies = {d: remote(head, head, ag1_s.at[d], ag1_r.at[d], at_z(d)) for d in far}
    ae_copies = {d: remote(age.at[z], age.at[z], ae_s.at[d], ae_r.at[d], at_z(d)) for d in far}
    az_copies = {d: remote(agz.at[h], agz.at[h], az_s.at[d], az_r.at[d], at_plane(d)) for d in far}
    ag2_copies = {
        d: remote(agp.at[used], gp.at[h, used], ag2_s.at[d], ag2_r.at[d], at_plane(d)) for d in far
    }
    ge_copies = {d: remote(age, ge.at[h], ge_s.at[d], ge_r.at[d], at_plane(d)) for d in far}
    gz_copies = {d: remote(agz, gz.at[z], gz_s.at[d], gz_r.at[d], at_z(d)) for d in far}
    own_copies = [
        pltpu.make_async_copy(agp, gp.at[h], in_s.at[12]),
        pltpu.make_async_copy(age, ge.at[h], in_s.at[13]),
        pltpu.make_async_copy(agz, gz.at[z], in_s.at[14]),
    ]
    for d in far:
        ag1_copies[d].start()
        ae_copies[d].start()
    for d in far:
        az_copies[d].start()
    for d in far:
        az_copies[d].wait_recv()

    @pl.when(z < 6)
    def _():
        for d in far:
            gz_copies[d].start()

    for d in far:
        ag1_copies[d].wait_recv()
        ae_copies[d].wait_recv()
    for d in far:
        ag2_copies[d].start()
        ge_copies[d].start()
    for copy in own_copies:
        copy.start()
    for d in far:
        ag2_copies[d].wait_recv()
        ge_copies[d].wait_recv()

        @pl.when((z + 8 - d) % 8 < 6)
        def _():
            gz_copies[d].wait_recv()

    for copy in own_copies:
        copy.wait()

    @pl.when(z < 6)
    def _():
        for d in far:
            gz_copies[d].wait_send()

    for copies in (rs2_copies, re_copies, ag1_copies, ae_copies, az_copies, ag2_copies, ge_copies):
        for copy in copies.values():
            copy.wait_send()
    for copy in rs1_copies:
        copy.wait_send()


def finish(head_ref, tail_ref, power_ref, frac_in, evid_in, out_ref, frac_ref, evid_ref, fin):
    for g in range(4):
        for zs in range(7):
            size = HEAD if zs < 6 else 16
            scale = jnp.exp2(power_ref[g, zs])
            code = head_ref[g, zs * HEAD : zs * HEAD + size].astype(jnp.int32).astype(F32)
            fin[zs * SLOT : zs * SLOT + size, :] = code * scale
            if zs < 6:
                code = tail_ref[zs, g].astype(jnp.int32).astype(F32)
                fin[zs * SLOT + HEAD : (zs + 1) * SLOT, :] = code * scale
        for n in range(12):
            at = g * 1536 + n * 128
            out_ref[:, at : at + 128] = fin[pl.ds(n, 25, stride=12), :]
    frac_ref[...] = frac_in[...]
    evid_ref[...] = evid_in[...]


def step(particles, references, centers, rot_prior, groups, class_frac, inv_noise, reg_inv):
    shift, center = tables()
    spread, rows = shard_maps()
    vmem = pl.BlockSpec(memory_space=pltpu.VMEM)
    dma = pltpu.SemaphoreType.DMA
    hbm = pl.BlockSpec(memory_space=pltpu.HBM)
    head, tail, power, frac, evid = pl.pallas_call(
        kernel,
        out_shape=(
            jax.ShapeDtypeStruct((8, 8 * HEAD, 128), jnp.int16),
            jax.ShapeDtypeStruct((8, 8, 16, 128), jnp.int16),
            jax.ShapeDtypeStruct((8, 8, 1, 128), F32),
            jax.ShapeDtypeStruct((1, 25), F32),
            jax.ShapeDtypeStruct((1, 2), F32),
        ),
        in_specs=[hbm] * 12,
        out_specs=(hbm, hbm, hbm, vmem, vmem),
        scratch_shapes=[
            pltpu.VMEM((2, FEAT), BF16),
            pltpu.SMEM((2, 2), jnp.int32),
            pltpu.SMEM((2,), jnp.int32),
            pltpu.SMEM((2,), jnp.int32),
            pltpu.VMEM((1, 100), F32),
            pltpu.VMEM((16, CYCLES), F32),
            pltpu.VMEM((1, CYCLES), F32),
            pltpu.VMEM((25, FEAT), BF16),
            pltpu.VMEM((12, 64, 512), F32),
            pltpu.VMEM((12, 16, 512), F32),
            pltpu.VMEM((128, 1024), BF16),
            pltpu.VMEM((SLOT, 8 * SLOT), BF16),
            pltpu.VMEM((16, 1536), F32),
            pltpu.VMEM((8, 128), F32),
            pltpu.VMEM((16, 1536), BF16),
            pltpu.VMEM((4, 16, 1536), BF16),
            pltpu.VMEM((4, 8, 128), F32),
            pltpu.VMEM((12 * 64, 128), F32),
            pltpu.VMEM((12, 8, 512), F32),
            pltpu.VMEM((12, 8, 512), F32),
            pltpu.VMEM((12 * 256, 1024), BF16),
            pltpu.VMEM((24 * 32, 1024), BF16),
            pltpu.VMEM((KPAD, 512), F32),
            pltpu.VMEM((384, 256), F32),
            pltpu.VMEM((16, 128), F32),
            pltpu.VMEM((4, 16, 128), F32),
            pltpu.VMEM((384, 12 * 256), BF16),
            pltpu.VMEM((384, 256), F32),
            pltpu.VMEM((2 * ROWS, 128), F32),
            pltpu.VMEM((8, ROWS, 128), jnp.int16),
            pltpu.VMEM((8, ROWS, 128), jnp.int16),
            pltpu.VMEM((ROWS, 128), F32),
            pltpu.VMEM((8 * SLOT, 128), F32),
            pltpu.VMEM((8 * SLOT, 128), jnp.int16),
            pltpu.VMEM((1, 128), F32),
            pltpu.VMEM((8, SLOT, 128), jnp.int16),
            pltpu.VMEM((8, 1, 128), F32),
            pltpu.VMEM((8 * HEAD, 128), jnp.int16),
            pltpu.VMEM((8, 16, 128), jnp.int16),
            pltpu.VMEM((8, 1, 128), F32),
            pltpu.VMEM((KPAD, 128), F32),
            pltpu.VMEM((KPAD, 128), F32),
            pltpu.VMEM((8, KPAD, 128), F32),
            pltpu.VMEM((KPAD, 128), F32),
            pltpu.VMEM((8, KPAD, 128), F32),
            dma((15,)),
        ]
        + [dma((4,))] * 6
        + [dma((8,))] * 6
        + [dma((8,))] * 16,
        compiler_params=pltpu.CompilerParams(
            collective_id=0, has_side_effects=True, vmem_limit_bytes=60 * 1024 * 1024
        ),
    )(
        particles, centers, rot_prior, groups, class_frac.reshape(1, 100), inv_noise,
        reg_inv.reshape(1, CYCLES), references, jnp.asarray(shift), jnp.asarray(center),
        jnp.asarray(spread, BF16), jnp.asarray(rows, BF16),
    )
    one = lambda shape: pl.BlockSpec(shape, lambda g: (0,) * len(shape))
    out, frac, evid = pl.pallas_call(
        finish,
        grid=(2,),
        out_shape=(
            jax.ShapeDtypeStruct((25, FEAT), F32),
            jax.ShapeDtypeStruct((1, 25), F32),
            jax.ShapeDtypeStruct((1, 2), F32),
        ),
        in_specs=[
            pl.BlockSpec((4, 8 * HEAD, 128), lambda g: (g, 0, 0)),
            pl.BlockSpec((8, 4, 16, 128), lambda g: (0, g, 0, 0)),
            pl.BlockSpec((4, 8, 1, 128), lambda g: (g, 0, 0, 0)),
            one((1, 25)),
            one((1, 2)),
        ],
        out_specs=(pl.BlockSpec((25, 6144), lambda g: (0, g)), one((1, 25)), one((1, 2))),
        scratch_shapes=[pltpu.VMEM((8 * SLOT, 128), F32)],
        compiler_params=pltpu.CompilerParams(vmem_limit_bytes=60 * 1024 * 1024),
    )(head, tail, power, frac, evid)
    return out, frac.reshape(25), evid.reshape(2)


def solution(mesh):
    both = ("cls", "ptl")
    return jax.shard_map(
        step,
        mesh=mesh,
        in_specs=(P(both, None), P("cls", None), P(both, None), P(both), P(both), P(), P(), P()),
        out_specs=(P("cls", None), P("cls"), P(both)),
        check_vma=False,
    )
```

```python
import math

import jax
import jax.numpy as jnp
import numpy as np
from jax import lax
from jax.experimental import pallas as pl
from jax.experimental.pallas import tpu as pltpu
from jax.sharding import PartitionSpec as P

ROTS = 12
SPAN = 2
CYCLES = 32
ANGLES = 192
BOX = 128
SHIFTS = 25
FEAT = 12288
KAPPA = 0.25
HIGHEST = lax.Precision.HIGHEST
MESH = pl.DeviceIdType.MESH
F32, BF16 = jnp.float32, jnp.bfloat16

KPAD = 32
ROWS = 304
HEAD = 32
SLOT = 48


def tables():
    cycle = np.arange(CYCLES, dtype=np.float64) + 1.0
    angle = np.arange(ANGLES, dtype=np.float64) * (2.0 * math.pi / ANGLES)
    fx = cycle[:, None] * np.cos(angle)[None] / BOX
    fy = cycle[:, None] * np.sin(angle)[None] / BOX

    def blocked(v):
        n = v.shape[0]
        v = v.reshape(n, 4, 8, 12, 16)
        return np.transpose(v, (3, 0, 1, 2, 4)).reshape(12, n, 512)

    t = np.arange(SHIFTS)
    mx, my = t // 5 - SPAN, t % 5 - SPAN
    ph = 2.0 * math.pi * (mx[:, None, None] * fx + my[:, None, None] * fy)
    shift = np.concatenate([np.cos(ph), np.zeros((7, 32, 192)), np.sin(ph), np.zeros((7, 32, 192))])
    rows = []
    for f in (fx, fy):
        for m in (1, 2, 3):
            rows += [np.cos(2.0 * math.pi * m * f), np.sin(2.0 * math.pi * m * f)]
    center = np.stack(rows + [np.zeros_like(fx)] * 4)
    return blocked(shift).astype(np.float32), blocked(center).astype(np.float32)


def shard_maps():
    spread = np.zeros((128, 1024), np.float32)
    for rho in range(8):
        for j in range(8):
            for s in range(16):
                spread[rho * 16 + s, rho * 128 + j * 16 + s] = 1
    rows = np.zeros((SLOT, 8 * SLOT), np.float32)
    for rho in range(8):
        for k in range(4):
            for b in range(12):
                rows[k * 12 + (12 * rho + b) // 8, rho * SLOT + k * 12 + b] = 1
    return spread, rows


def to_blocks(nat):
    lane = lax.broadcasted_iota(jnp.int32, nat[0].shape, 1) // 16
    out = []
    for b in range(12):
        acc = None
        for rho in range(8):
            n, j = divmod(12 * rho + b, 8)
            v = nat[n] if j == rho else pltpu.roll(nat[n], (16 * (rho - j)) % 128, 1)
            acc = v if acc is None else jnp.where(lane == rho, v, acc)
        out.append(acc)
    return out


def fold(v, op):
    v = jnp.broadcast_to(op(v[:, :128], v[:, 128:]), (8, 128))
    for step in (8, 16, 32, 64):
        v = op(v, pltpu.roll(v, step, 1))
    return v


def encode(value, to):
    top = jnp.max(jnp.abs(value), axis=0, keepdims=True)
    power = jnp.ceil(jnp.log2(jnp.maximum(top, 1e-30)) + 1e-3) - 15.0
    code = jnp.round(value * jnp.exp2(-power))
    row = lax.broadcasted_iota(jnp.int32, value.shape, 0)
    to[...] = jnp.where(row == 300, power, code).astype(jnp.int32).astype(jnp.int16)


def decode(code):
    value = code[...].astype(jnp.int32).astype(F32)
    return value * jnp.exp2(value[300:301])


def encode_rows(value):
    top = jnp.max(jnp.abs(value), axis=0, keepdims=True)
    power = jnp.ceil(jnp.log2(jnp.maximum(top, 1e-30)) + 1e-3) - 15.0
    code = jnp.round(value * jnp.exp2(-power)).astype(jnp.int32).astype(jnp.int16)
    return code, power


def kernel(
    x_hbm, cen_hbm, rot_hbm, group_hbm, frac_hbm, noise_hbm, reg_hbm,
    refs_hbm, shift_hbm, center_hbm, spread_hbm, rows_hbm,
    gp, gz, ge, frac_ref, evid_ref,
    x_ref, cen_ref, rot_ref, group_ref, frac_in, noise_ref, reg_ref,
    refs_ref, shift_ref, center_ref, spread_ref, rows_ref,
    xs, ms, xb, xg, mg, xf, yre, yim, a_ref, r2, pw, s_ref, sm_src, sm, p2, n_ref, nb, sb, rs1, acc,
    ph2, ph2c, ph2e, rs2, rs2e, agp, agz, age, fin, dsrc, dz, dpsrc, dp, in_s,
    x_s, x_r, m_s, m_r, sm_s, sm_r, rs1_s, rs1_r, rs2_s, rs2_r, ag1_s, ag1_r, ag2_s, ag2_r, re_s, re_r, ae_s, ae_r, ge_s, ge_r,
    az_s, az_r, gz_s, gz_r,
    dz_s, dz_r, dp_s, dp_r,
):
    c = lax.axis_index("cls")
    q = lax.axis_index("ptl")
    h, z = q // 8, q % 8

    def at_cls(d):
        return ((c + d) % 4, q)

    def at_z(d):
        return (c, h * 8 + (z + d) % 8)

    def at_plane(d):
        return (c, ((h + d) % 8) * 8 + z)

    loads = [
        pltpu.make_async_copy(src, dst, in_s.at[i])
        for i, (src, dst) in enumerate(
            (
                (refs_hbm, refs_ref), (center_hbm, center_ref), (shift_hbm, shift_ref),
                (spread_hbm, spread_ref), (rows_hbm, rows_ref),
                (frac_hbm, frac_in), (reg_hbm, reg_ref),
                (cen_hbm, cen_ref), (rot_hbm, rot_ref), (group_hbm, group_ref),
                (noise_hbm, noise_ref), (x_hbm, x_ref),
            )
        )
    ]
    for load in loads[::-1]:
        load.start()
    barrier = pltpu.get_barrier_semaphore()
    for d in range(1, 4):
        pl.semaphore_signal(barrier, inc=1, device_id=at_cls(d), device_id_type=MESH)
    for d in range(1, 8):
        pl.semaphore_signal(barrier, inc=1, device_id=at_z(d), device_id_type=MESH)
        pl.semaphore_signal(barrier, inc=1, device_id=at_plane(d), device_id_type=MESH)

    lane1 = lax.broadcasted_iota(jnp.int32, (1, 128), 1)
    ms[...] = jnp.zeros_like(ms)
    for load in loads[7:]:
        load.wait()
    for p in range(2):
        for g in range(8):
            xs[p * 8 + g : p * 8 + g + 1, :] = x_ref[p : p + 1, g * 1536 : (g + 1) * 1536].astype(F32)
        group = lax.broadcasted_iota(jnp.int32, (16, CYCLES), 0) == group_ref[p]
        inv = jnp.sum(jnp.where(group, noise_ref[...], 0.0), axis=0, keepdims=True)
        info = jnp.concatenate([inv, jnp.ones((1, 96), F32)], axis=1)
        for at, value in ((40, cen_ref[p, 0]), (41, cen_ref[p, 1]), (42, rot_ref[p])):
            info = jnp.where(lane1 == at, value.astype(F32), info)
        ms[p * 4 : p * 4 + 1, :] = info
    xb[...] = xs[...].astype(BF16)
    xg[c] = xb[...]
    mg[c] = ms[...]

    def remote(src, dst, ss, rs, dev):
        return pltpu.make_async_remote_copy(
            src_ref=src, dst_ref=dst, send_sem=ss, recv_sem=rs, device_id=dev, device_id_type=MESH
        )

    pl.semaphore_wait(barrier, 17)

    x_copies = []
    for d in range(1, 4):
        x_copies.append(remote(ms, mg.at[c], m_s.at[d], m_r.at[d], at_cls(d)))
        x_copies.append(remote(xb, xg.at[c], x_s.at[d], x_r.at[d], at_cls(d)))
    for copy in x_copies:
        copy.start()

    pw[...] = jnp.zeros_like(pw)
    loads[0].wait()

    def one_group(g, carry):
        at = pl.multiple_of(g * 1536, 1536)
        nat = [refs_ref[:, pl.ds(at + n * 128, 128)].astype(F32) for n in range(12)]
        blocks = to_blocks(nat)
        power = blocks[0] * blocks[0]
        for b in range(1, 12):
            power = power + blocks[b] * blocks[b]
        to = pl.multiple_of(g * 128, 128)
        pw[0:25, pl.ds(pl.multiple_of((g % 4) * 128, 128), 128)] += power
        for b in range(12):
            v = blocks[b].astype(BF16)
            j = (12 - b) % 12
            r2[j * 32 : j * 32 + 25, pl.ds(to, 128)] = v
            r2[(j + 12) * 32 : (j + 12) * 32 + 25, pl.ds(to, 128)] = v
        return carry

    lax.fori_loop(0, 8, one_group, 0)
    for b in range(12):
        a_ref[b * 256 + 192 : b * 256 + 256, :] = jnp.zeros((64, 1024), BF16)
    nb[...] = jnp.zeros_like(nb)
    ph2[...] = jnp.zeros_like(ph2)
    ph2c[...] = jnp.zeros_like(ph2c)
    for load in loads[1:7]:
        load.wait()
    for copy in x_copies:
        copy.wait()

    for i in range(4):
        for n in range(12):
            at = n * 64 + i * 16
            xf[at : at + 16, :] = xg[i, :, n * 128 : n * 128 + 128].astype(F32)
    for i in range(4):
        fin[i * 8 : i * 8 + 8, :] = mg[i]
    info = fin[pl.ds(0, 8, stride=4), :]
    lane8 = lax.broadcasted_iota(jnp.int32, (8, 128), 1)
    cx, cy = info[:, 40:41], info[:, 41:42]
    turn = jnp.where(lane8 % 8 == lax.broadcasted_iota(jnp.int32, (8, 128), 0), info[:, 42:43], 0.0)
    turn = jnp.sum(turn, axis=0, keepdims=True)
    grow = (
        lax.broadcasted_iota(jnp.int32, (CYCLES, 512), 0)
        == lax.broadcasted_iota(jnp.int32, (CYCLES, 512), 1) // 16
    ).astype(F32)
    w512 = jnp.dot(info[:, 0:CYCLES], grow, preferred_element_type=F32, precision=HIGHEST)
    w = [w512[:, i * 128 : i * 128 + 128] for i in range(4)]

    def phase(value, row, b, gq):
        size = jnp.abs(value)
        cos, sin = jnp.ones((8, 128), F32), jnp.zeros((8, 128), F32)
        for m in (1, 2, 3):
            hit = size == float(m)
            at = row + (m - 1) * 2
            cos = jnp.where(hit, center_ref[b, at : at + 1, gq * 128 : gq * 128 + 128], cos)
            sin = jnp.where(hit, center_ref[b, at + 1 : at + 2, gq * 128 : gq * 128 + 128], sin)
        return cos, jnp.where(value < 0.0, -sin, sin)

    for gq in range(4):
        re = to_blocks([xf[pl.ds(n * 64 + gq, 8, stride=8), :] for n in range(12)])
        im = to_blocks([xf[pl.ds(n * 64 + gq + 4, 8, stride=8), :] for n in range(12)])
        for b in range(12):
            xc, xs = phase(cx, 0, b, gq)
            yc, ys = phase(cy, 6, b, gq)
            pc, ps = xc * yc - xs * ys, xc * ys + xs * yc
            u, v = re[b] * w[gq], im[b] * w[gq]
            yre[b, :, gq * 128 : gq * 128 + 128] = u * pc - v * ps
            yim[b, :, gq * 128 : gq * 128 + 128] = u * ps + v * pc

    def align(b):
        for l in range(4):
            cols = slice(l * 128, l * 128 + 128)
            u, v = yre[b, :, cols], yim[b, :, cols]
            for t in range(0, 25, 2):
                res, ims = [], []
                for tt in range(t, min(t + 2, 25)):
                    tc = shift_ref[b, tt : tt + 1, cols]
                    ts = shift_ref[b, 32 + tt : 33 + tt, cols]
                    res.append(u * tc - v * ts)
                    ims.append(u * ts + v * tc)
                if len(res) == 1:
                    res.append(jnp.zeros((8, 128), F32))
                    ims.append(jnp.zeros((8, 128), F32))
                at = slice(b * 256 + t * 8, b * 256 + t * 8 + 16)
                a_ref[at, cols] = jnp.concatenate(res, axis=0).astype(BF16)
                a_ref[at, l * 128 + 512 : l * 128 + 640] = jnp.concatenate(ims, axis=0).astype(BF16)

    def score(b):
        row = ((12 - b) % 12) * 32
        part = lax.dot_general(
            r2[row : row + 384, :], a_ref[b * 256 : b * 256 + 256, :],
            (((1,), (1,)), ((), ())), preferred_element_type=F32,
        )
        if b == 0:
            s_ref[...] = part
        else:
            s_ref[...] += part

    align(0)
    for b in range(12):
        if b < 11:
            align(b + 1)
        score(b)

    w128 = jnp.concatenate([w512] * 16, axis=0)
    pen = lax.dot_general(
        pw[...], w128, (((1,), (1,)), ((), ())), preferred_element_type=F32, precision=HIGHEST
    )
    mine = (
        lax.broadcasted_iota(jnp.int32, (KPAD, 100), 0) + c * 25
        == lax.broadcasted_iota(jnp.int32, (KPAD, 100), 1)
    )
    frac = jnp.sum(jnp.where(mine, frac_in[...], 0.0), axis=1, keepdims=True)
    base = jnp.log(jnp.where(frac > 0.0, frac, 1.0)) - 0.5 * pen
    base = jnp.concatenate([base, base], axis=1)
    away = lax.broadcasted_iota(jnp.int32, (16, 128), 0).astype(F32) - turn
    away = jnp.where(away < 0.0, away + 12.0, away)
    away = jnp.minimum(away, 12.0 - away)
    prior = -KAPPA * away * away
    prior = jnp.concatenate([prior, prior], axis=1)
    live = (lax.broadcasted_iota(jnp.int32, (KPAD, 256), 0) < 25) & (
        lax.broadcasted_iota(jnp.int32, (KPAD, 256), 1) < 200
    )
    top = jnp.full((KPAD, 256), -3e38, F32)
    for r in range(12):
        v = s_ref[r * 32 : r * 32 + 32, :] + (base + prior[r : r + 1, :])
        v = jnp.where(live, v, -3e38)
        s_ref[r * 32 : r * 32 + 32, :] = v
        top = jnp.maximum(top, v)
    here = fold(jnp.max(top, axis=0, keepdims=True), jnp.maximum)
    here256 = jnp.concatenate([here, here], axis=1)[0:1]
    total = jnp.zeros((KPAD, 256), F32)
    for r in range(12):
        v = jnp.where(live, jnp.exp(s_ref[r * 32 : r * 32 + 32, :] - here256), 0.0)
        s_ref[r * 32 : r * 32 + 32, :] = v
        total = total + v
    mass = fold(jnp.sum(total, axis=0, keepdims=True), jnp.add)
    sm_src[0:8] = here
    sm_src[8:16] = mass
    sm_copies = [remote(sm_src, sm.at[d], sm_s.at[d], sm_r.at[d], at_cls(d)) for d in range(1, 4)]
    for copy in sm_copies:
        copy.start()
    for copy in sm_copies:
        copy.wait()
    peak = here
    for d in range(1, 4):
        peak = jnp.maximum(peak, sm[d, 0:8])
    full = mass * jnp.exp(here - peak)
    for d in range(1, 4):
        full = full + sm[d, 8:16] * jnp.exp(sm[d, 0:8] - peak)
    evid = (peak + jnp.log(full))[0:1]
    first = jnp.sum(jnp.where(lane1 == 2 * c, evid, 0.0), axis=1, keepdims=True)
    second = jnp.sum(jnp.where(lane1 == 2 * c + 1, evid, 0.0), axis=1, keepdims=True)
    evid_ref[...] = jnp.where(lane1 == 0, first, second)[:, 0:2]
    scale = jnp.exp(here - peak) / full
    scale256 = jnp.concatenate([scale, scale], axis=1)[0:1]
    weight = jnp.zeros((KPAD, 256), F32)
    for r in range(12):
        v = s_ref[r * 32 : r * 32 + 32, :] * scale256
        weight = weight + v
        v = v.astype(BF16)
        for b1 in range(12):
            b = (b1 - r) % 12
            p2[b * 32 : b * 32 + 32, b1 * 256 : b1 * 256 + 256] = v

    inv256 = jnp.concatenate([info] * 32, axis=0)
    dsrc[...] = lax.dot_general(
        weight, inv256, (((1,), (0,)), ((), ())), preferred_element_type=F32, precision=HIGHEST
    )
    dz_copies = [remote(dsrc, dz.at[d], dz_s.at[d], dz_r.at[d], at_z(d)) for d in range(1, 8)]
    for copy in dz_copies:
        copy.start()

    def weighted(*steps):
        offs = [pl.multiple_of(((h + d) % 8) * 128, 128) for d in steps]
        rhs = jnp.concatenate([a_ref[:, pl.ds(o, 128)] for o in offs], axis=1)
        n_ref[...] = jnp.dot(p2[...], rhs, preferred_element_type=F32)
        for e in range(2):
            for b in range(12):
                nb[pl.ds(e * ROWS + b, 25, stride=12), :] = n_ref[
                    b * 32 : b * 32 + 25, e * 128 : e * 128 + 128
                ]

    def rs1_copy(d):
        return remote(sb.at[d], rs1.at[d], rs1_s.at[d], rs1_r.at[d], at_plane(d))

    def send_sum(d, e):
        encode(nb[e * ROWS : e * ROWS + ROWS, :], sb.at[d])
        rs1_copy(d).start()

    def one_pair(i, carry):
        late = (i * (i - 1)) // 2
        one, two = 6 - 4 * i + 9 * late, 5 - i - 2 * late
        weighted(one, two)
        send_sum(one, 0)
        send_sum(two, 1)
        return carry

    lax.fori_loop(0, 3, one_pair, 0)
    weighted(3, 8)
    send_sum(3, 0)
    acc[...] = nb[ROWS : 2 * ROWS, :]
    rs1_copies = [rs1_copy(d) for d in range(1, 8)]

    for copy in dz_copies:
        copy.wait()
    dsum = dsrc[...]
    for d in range(1, 8):
        dsum = dsum + dz[d]
    dpsrc[...] = dsum
    dp_copies = [remote(dpsrc, dp.at[d], dp_s.at[d], dp_r.at[d], at_plane(d)) for d in range(1, 8)]
    for copy in dp_copies:
        copy.start()

    tot = acc[...]
    for d in (6, 5, 2, 4, 7, 1, 3):
        rs1_copies[d - 1].wait_recv()
        tot = tot + decode(rs1.at[d])
    tot = jnp.where(lax.broadcasted_iota(jnp.int32, (ROWS, 128), 0) < 300, tot, 0.0)
    ph2[0:ROWS, :] = tot
    code, power = encode_rows(tot)
    ph2c[0:ROWS, :] = code
    ph2e[...] = power

    far = (4, 3, 5, 2, 6, 1, 7)
    re_copies = {d: remote(ph2e, rs2e.at[d], re_s.at[d], re_r.at[d], at_z(d)) for d in far}
    rs2_copies = {}
    for d in far:
        at = pl.multiple_of(((z + d) % 8) * SLOT, 16)
        rs2_copies[d] = remote(
            ph2c.at[pl.ds(at, SLOT)], rs2.at[d], rs2_s.at[d], rs2_r.at[d], at_z(d)
        )
        rs2_copies[d].start()
        re_copies[d].start()
    for copy in dp_copies:
        copy.wait()
    dsum = dpsrc[...]
    for d in range(1, 8):
        dsum = dsum + dp[d]
    square = (
        lax.broadcasted_iota(jnp.int32, (KPAD, KPAD), 0)
        == lax.broadcasted_iota(jnp.int32, (KPAD, KPAD), 1)
    )
    frac = jnp.sum(jnp.where(square, dsum[:, 32:33], 0.0), axis=0, keepdims=True)
    frac_ref[...] = frac[:, 0:25] * (1.0 / 512.0)
    rho = lax.broadcasted_iota(jnp.int32, (CYCLES, 128), 0)
    lane = lax.broadcasted_iota(jnp.int32, (CYCLES, 128), 1)
    pick = (rho == (h % 4) * 8 + lane // 16).astype(F32)
    mine = lax.broadcasted_iota(jnp.int32, (SLOT, KPAD), 0) // 12 + z * 4
    mine = (mine == lax.broadcasted_iota(jnp.int32, (SLOT, KPAD), 1)).astype(F32)
    div = jnp.dot(dsum[:, 0:CYCLES] + reg_ref[...], pick, preferred_element_type=F32, precision=HIGHEST)
    div = jnp.dot(mine, div, preferred_element_type=F32, precision=HIGHEST)
    own = pl.multiple_of(z * SLOT, 16)
    tot = ph2[pl.ds(own, SLOT), :]
    for d in range(1, 8):
        rs2_copies[d].wait_recv()
        re_copies[d].wait_recv()
        tot = tot + rs2[d].astype(jnp.int32).astype(F32) * jnp.exp2(rs2e[d])
    inside = lax.broadcasted_iota(jnp.int32, (SLOT, 128), 0) // 12 + z * 4 < 25
    tot = jnp.where(inside, tot / jnp.where(inside, div, 1.0), 0.0)

    high = tot.astype(BF16)
    low = (tot - high.astype(F32)).astype(BF16)
    wide = jnp.dot(jnp.concatenate([high, low], axis=0), spread_ref[...], preferred_element_type=F32)
    brow = lax.broadcasted_iota(jnp.int32, (SLOT, 128), 0) % 12
    slot = lax.broadcasted_iota(jnp.int32, (SLOT, 128), 1) // 16
    stack = jnp.concatenate(
        [
            jnp.concatenate(
                [
                    jnp.where(
                        slot == (4 * r + brow) % 8,
                        wide[i * SLOT : (i + 1) * SLOT, r * 128 : r * 128 + 128],
                        0.0,
                    )
                    for i in range(2)
                ],
                axis=1,
            )
            for r in range(8)
        ],
        axis=0,
    ).astype(BF16)
    both = jnp.dot(rows_ref[...], stack, preferred_element_type=F32)
    code, power = encode_rows(both[:, 0:128] + both[:, 128:256])
    first = pl.multiple_of(z * HEAD, HEAD)
    agp[pl.ds(first, HEAD), :] = code[0:HEAD]
    agz[h] = code[HEAD:SLOT]
    age[z] = power

    head = agp.at[pl.ds(first, HEAD)]
    used = pl.ds(0, 6 * HEAD + 16)
    ag1_copies = {d: remote(head, head, ag1_s.at[d], ag1_r.at[d], at_z(d)) for d in far}
    ae_copies = {d: remote(age.at[z], age.at[z], ae_s.at[d], ae_r.at[d], at_z(d)) for d in far}
    az_copies = {d: remote(agz.at[h], agz.at[h], az_s.at[d], az_r.at[d], at_plane(d)) for d in far}
    ag2_copies = {
        d: remote(agp.at[used], gp.at[h, used], ag2_s.at[d], ag2_r.at[d], at_plane(d)) for d in far
    }
    ge_copies = {d: remote(age, ge.at[h], ge_s.at[d], ge_r.at[d], at_plane(d)) for d in far}
    gz_copies = {d: remote(agz, gz.at[z], gz_s.at[d], gz_r.at[d], at_z(d)) for d in far}
    own_copies = [
        pltpu.make_async_copy(agp, gp.at[h], in_s.at[12]),
        pltpu.make_async_copy(age, ge.at[h], in_s.at[13]),
        pltpu.make_async_copy(agz, gz.at[z], in_s.at[14]),
    ]
    for d in far:
        ag1_copies[d].start()
        ae_copies[d].start()
    for d in far:
        az_copies[d].start()
    for d in far:
        az_copies[d].wait_recv()

    @pl.when(z < 6)
    def _():
        for d in far:
            gz_copies[d].start()

    for d in far:
        ag1_copies[d].wait_recv()
        ae_copies[d].wait_recv()
    for d in far:
        ag2_copies[d].start()
        ge_copies[d].start()
    for copy in own_copies:
        copy.start()
    for d in far:
        ag2_copies[d].wait_recv()
        ge_copies[d].wait_recv()

        @pl.when((z + 8 - d) % 8 < 6)
        def _():
            gz_copies[d].wait_recv()

    for copy in own_copies:
        copy.wait()

    @pl.when(z < 6)
    def _():
        for d in far:
            gz_copies[d].wait_send()

    for copies in (rs2_copies, re_copies, ag1_copies, ae_copies, az_copies, ag2_copies, ge_copies):
        for copy in copies.values():
            copy.wait_send()
    for copy in rs1_copies:
        copy.wait_send()


def finish(head_ref, tail_ref, power_ref, frac_in, evid_in, out_ref, frac_ref, evid_ref, fin):
    for g in range(4):
        for zs in range(7):
            size = HEAD if zs < 6 else 16
            scale = jnp.exp2(power_ref[g, zs])
            code = head_ref[g, zs * HEAD : zs * HEAD + size].astype(jnp.int32).astype(F32)
            fin[zs * SLOT : zs * SLOT + size, :] = code * scale
            if zs < 6:
                code = tail_ref[zs, g].astype(jnp.int32).astype(F32)
                fin[zs * SLOT + HEAD : (zs + 1) * SLOT, :] = code * scale
        for n in range(12):
            at = g * 1536 + n * 128
            out_ref[:, at : at + 128] = fin[pl.ds(n, 25, stride=12), :]
    frac_ref[...] = frac_in[...]
    evid_ref[...] = evid_in[...]


def step(particles, references, centers, rot_prior, groups, class_frac, inv_noise, reg_inv):
    shift, center = tables()
    spread, rows = shard_maps()
    vmem = pl.BlockSpec(memory_space=pltpu.VMEM)
    dma = pltpu.SemaphoreType.DMA
    hbm = pl.BlockSpec(memory_space=pltpu.HBM)
    head, tail, power, frac, evid = pl.pallas_call(
        kernel,
        out_shape=(
            jax.ShapeDtypeStruct((8, 8 * HEAD, 128), jnp.int16),
            jax.ShapeDtypeStruct((8, 8, 16, 128), jnp.int16),
            jax.ShapeDtypeStruct((8, 8, 1, 128), F32),
            jax.ShapeDtypeStruct((1, 25), F32),
            jax.ShapeDtypeStruct((1, 2), F32),
        ),
        in_specs=[hbm] * 12,
        out_specs=(hbm, hbm, hbm, vmem, vmem),
        scratch_shapes=[
            pltpu.VMEM((2, FEAT), BF16),
            pltpu.SMEM((2, 2), jnp.int32),
            pltpu.SMEM((2,), jnp.int32),
            pltpu.SMEM((2,), jnp.int32),
            pltpu.VMEM((1, 100), F32),
            pltpu.VMEM((16, CYCLES), F32),
            pltpu.VMEM((1, CYCLES), F32),
            pltpu.VMEM((25, FEAT), BF16),
            pltpu.VMEM((12, 64, 512), F32),
            pltpu.VMEM((12, 16, 512), F32),
            pltpu.VMEM((128, 1024), BF16),
            pltpu.VMEM((SLOT, 8 * SLOT), BF16),
            pltpu.VMEM((16, 1536), F32),
            pltpu.VMEM((8, 128), F32),
            pltpu.VMEM((16, 1536), BF16),
            pltpu.VMEM((4, 16, 1536), BF16),
            pltpu.VMEM((4, 8, 128), F32),
            pltpu.VMEM((12 * 64, 128), F32),
            pltpu.VMEM((12, 8, 512), F32),
            pltpu.VMEM((12, 8, 512), F32),
            pltpu.VMEM((12 * 256, 1024), BF16),
            pltpu.VMEM((24 * 32, 1024), BF16),
            pltpu.VMEM((KPAD, 512), F32),
            pltpu.VMEM((384, 256), F32),
            pltpu.VMEM((16, 128), F32),
            pltpu.VMEM((4, 16, 128), F32),
            pltpu.VMEM((384, 12 * 256), BF16),
            pltpu.VMEM((384, 256), F32),
            pltpu.VMEM((2 * ROWS, 128), F32),
            pltpu.VMEM((8, ROWS, 128), jnp.int16),
            pltpu.VMEM((8, ROWS, 128), jnp.int16),
            pltpu.VMEM((ROWS, 128), F32),
            pltpu.VMEM((8 * SLOT, 128), F32),
            pltpu.VMEM((8 * SLOT, 128), jnp.int16),
            pltpu.VMEM((1, 128), F32),
            pltpu.VMEM((8, SLOT, 128), jnp.int16),
            pltpu.VMEM((8, 1, 128), F32),
            pltpu.VMEM((8 * HEAD, 128), jnp.int16),
            pltpu.VMEM((8, 16, 128), jnp.int16),
            pltpu.VMEM((8, 1, 128), F32),
            pltpu.VMEM((KPAD, 128), F32),
            pltpu.VMEM((KPAD, 128), F32),
            pltpu.VMEM((8, KPAD, 128), F32),
            pltpu.VMEM((KPAD, 128), F32),
            pltpu.VMEM((8, KPAD, 128), F32),
            dma((15,)),
        ]
        + [dma((4,))] * 6
        + [dma((8,))] * 6
        + [dma((8,))] * 16,
        compiler_params=pltpu.CompilerParams(
            collective_id=0, has_side_effects=True, vmem_limit_bytes=60 * 1024 * 1024
        ),
    )(
        particles, centers, rot_prior, groups, class_frac.reshape(1, 100), inv_noise,
        reg_inv.reshape(1, CYCLES), references, jnp.asarray(shift), jnp.asarray(center),
        jnp.asarray(spread, BF16), jnp.asarray(rows, BF16),
    )
    one = lambda shape: pl.BlockSpec(shape, lambda g: (0,) * len(shape))
    out, frac, evid = pl.pallas_call(
        finish,
        grid=(2,),
        out_shape=(
            jax.ShapeDtypeStruct((25, FEAT), F32),
            jax.ShapeDtypeStruct((1, 25), F32),
            jax.ShapeDtypeStruct((1, 2), F32),
        ),
        in_specs=[
            pl.BlockSpec((4, 8 * HEAD, 128), lambda g: (g, 0, 0)),
            pl.BlockSpec((8, 4, 16, 128), lambda g: (0, g, 0, 0)),
            pl.BlockSpec((4, 8, 1, 128), lambda g: (g, 0, 0, 0)),
            one((1, 25)),
            one((1, 2)),
        ],
        out_specs=(pl.BlockSpec((25, 6144), lambda g: (0, g)), one((1, 25)), one((1, 2))),
        scratch_shapes=[pltpu.VMEM((8 * SLOT, 128), F32)],
        compiler_params=pltpu.CompilerParams(vmem_limit_bytes=60 * 1024 * 1024),
    )(head, tail, power, frac, evid)
    return out, frac.reshape(25), evid.reshape(2)


def solution(mesh):
    both = ("cls", "ptl")
    return jax.shard_map(
        step,
        mesh=mesh,
        in_specs=(P(both, None), P("cls", None), P(both, None), P(both), P(both), P(), P(), P()),
        out_specs=(P("cls", None), P("cls"), P(both)),
        check_vma=False,
    )
```
